256 devices in a mesh: row: 32 (over z, x_hi, core), col: 8 (over y, x_lo).
Axes of the slice: x: 4 (x_hi: 2, x_lo: 2; x = x_hi * 2 + x_lo), y: 4, z: 8, core: 2. Of those that a mesh axis runs over, the one named last changes fastest.
Arguments:
- density: bfloat16 [12288, 12288], P('col', 'row'), may hold values from -1.5 to 1.5
- block_mask: int32 [96, 96], replicated, may hold values from 0 to 1, as said below
- owner: int32 [4, 8], replicated, may hold values from 0 to 31, as said below
Outputs:
- square_part: float32 [12288, 12288], P('col', 'row')
The draws below stay inside these ranges and needn't reach their ends.
Inputs may be any that keep to these rules, and one draw needn't show every extreme that they name: owner[t, g] // 4 equals (g + t) mod 8. `block_mask`: each tile of 12 x 3 blocks (block rows g * 12 onward, block columns j * 3 onward) has at most 21 entries equal to 1, and in every draw some tile has exactly 21.
All inputs are finite; a program needn't handle non-finite values.
Results may differ from the reference program's by a relative error of at most 0.0003.
Values may be sent and summed in bfloat16 or wider, within the bound.
A program may use at most 64 MiB of HBM per device.

```python
import jax
import jax.numpy as jnp
from jax import lax

BLOCK = 128
TC = 3
STEPS = 4
SUB = 4
TR = 12
CAP = 21
ORDER = 12288
N_ROW = 32
N_COL = 8


def draw_block_mask(key, part):
    key = jax.random.fold_in(key, 11)
    tiles = N_COL * N_ROW
    cells = TR * TC
    key_count, key_full, key_place = jax.random.split(key, 3)
    halvings = jax.random.randint(key_count, (tiles,), 0, 4)
    counts = CAP // jnp.left_shift(jnp.ones((tiles,), jnp.int32), halvings)
    fullest = jax.random.randint(key_full, (), 0, tiles)
    counts = jnp.where(jnp.arange(tiles) == fullest, CAP, counts)
    scores = jax.random.randint(key_place, (tiles, cells), 0, 1 << 20) * cells + jnp.arange(cells)[None, :]
    ranks = jnp.argsort(jnp.argsort(scores, axis=1), axis=1)
    flags = (ranks < counts[:, None]).astype(jnp.int32)
    flags = flags.reshape(N_COL, N_ROW, TR, TC).transpose(0, 2, 1, 3)
    return flags.reshape(N_COL * TR, N_ROW * TC)


def draw_owner(key, part):
    key = jax.random.fold_in(key, 23)
    sections = jnp.arange(STEPS, dtype=jnp.int32)[:, None]
    grid_rows = jnp.arange(N_COL, dtype=jnp.int32)[None, :]
    picks = jax.random.randint(key, (STEPS, N_COL), 0, SUB)
    first_section = sections == 0
    picks = jnp.where(first_section & (grid_rows == 0), 0, picks)
    picks = jnp.where(first_section & (grid_rows == N_COL - 1), SUB - 1, picks)
    return (SUB * ((grid_rows + sections) % N_COL) + picks).astype(jnp.int32)


def block_levels(stream_key, dims, shards, least, largest):
    def one(position, shards_of):
        heights = jax.random.uniform(jax.random.fold_in(jax.random.fold_in(stream_key, 6), position), (shards_of,), jnp.float32, least / len(shards), largest / len(shards))
        return jnp.repeat(jnp.exp(heights), dims[position] // shards_of).reshape((-1,) + (1,) * (len(dims) - position - 1))

    level = one(*shards[0])
    for cut in shards[1:]:
        level = level * one(*cut)
    return level


def normal_values(rng, shape, spread, reach, cuts=(), kind=jnp.bfloat16):
    loudness = block_levels(rng, shape, cuts, -0.22, 0.18) if cuts else 1.0
    array = jax.random.normal(rng, shape, jnp.float32) * spread * loudness
    return jnp.minimum(jnp.maximum(array, -reach), reach).astype(kind)


def setup_inputs(seed: int = 0) -> dict:
    streams_of = jax.random.split(jax.random.key(seed), 4)
    density = normal_values(streams_of[0], (ORDER, ORDER), 0.25, 1.5, ((0, 8), (1, 32)))
    block_mask = draw_block_mask(jax.random.fold_in(streams_of[3], 71), 0)
    owner = draw_owner(jax.random.fold_in(streams_of[3], 71), 0)
    return {"density": density, "block_mask": block_mask, "owner": owner}


def masked_matrix(density, block_mask):
    blocks_down = block_mask.shape[0]
    blocks_across = block_mask.shape[1]
    shaped = density.reshape(blocks_down, BLOCK, blocks_across, BLOCK)
    kept = jnp.where(block_mask[:, None, :, None] == 1, shaped, jnp.zeros((), jnp.bfloat16))
    return kept.reshape(density.shape)


def reference(density, block_mask, owner):
    masked = masked_matrix(density, block_mask)
    slab_rows = ORDER // N_COL
    slab_width = TC * BLOCK

    def one_slab(grid_row):
        offset_rows = (grid_row * slab_rows).astype(jnp.int32)
        rows_here = lax.dynamic_slice_in_dim(masked, offset_rows, slab_rows, 0)
        accumulated = jnp.zeros((slab_rows, ORDER), jnp.float32)
        for section_index in range(STEPS):
            offset = (owner[section_index, grid_row] * slab_width).astype(jnp.int32)
            left_tile = lax.dynamic_slice_in_dim(rows_here, offset, slab_width, 1)
            right_rows = lax.dynamic_slice_in_dim(masked, offset, slab_width, 0)
            accumulated = accumulated + jnp.dot(left_tile, right_rows, preferred_element_type=jnp.float32)
        return accumulated

    all_slabs = lax.map(one_slab, jnp.arange(N_COL, dtype=jnp.int32))
    return all_slabs.reshape(ORDER, ORDER)
```

```python
import functools

import jax
import jax.numpy as jnp
from jax import lax
from jax.experimental import pallas as pl
from jax.experimental.pallas import tpu as pltpu
from jax.sharding import PartitionSpec as P

BLOCK = 128
STEPS = 4
CAP = 21
HALF = BLOCK // 2
CHUNKS = 7
SPAN = CAP // CHUNKS
LAG = 3
MESH = pl.DeviceIdType.MESH


def kernel(
    n_row, n_col, density, mask, owner, out,
    tile, nxt, slots, packed, chosen, crossed, near, far, r_send, r_all, wide,
    load_sem, swap_s, swap_r, cross_s, cross_r, up_s, down_s, ring_r, mate_s, mate_r, slab_s, slab_r,
):
    g = lax.axis_index("col")
    j = lax.axis_index("row")
    sub = n_row // n_col
    planes = n_col
    plane = j // sub
    place = lax.rem(j, sub)
    core = lax.rem(place, 2)
    rel = lax.rem(plane - g + planes, planes)
    is_source = rel < STEPS
    row_blocks, _, width = density.shape
    col_blocks = width // BLOCK

    def at_plane(by):
        return {"col": g, "row": lax.rem(plane + by + planes, planes) * sub + place}

    def at_grid_row(by):
        return {"col": lax.rem(g + by + n_col, n_col), "row": j}

    mate = {"col": g, "row": plane * sub + place + 1 - 2 * core}
    across = {"col": g, "row": plane * sub + lax.rem(place + 2, sub)}

    barrier = pltpu.get_barrier_semaphore()
    senders = [mate, across, at_plane(1), at_plane(-1)] + [at_grid_row(t) for t in range(1, STEPS)]
    for device in senders:
        pl.semaphore_signal(barrier, inc=1, device_id=device, device_id_type=MESH)

    loads = [
        pltpu.make_async_copy(
            density.at[:, :, pl.ds(b * BLOCK, BLOCK)], tile.at[b, pl.ds(0, row_blocks)], load_sem.at[b]
        )
        for b in range(col_blocks)
    ]
    for load in loads:
        load.start()
    for b in range(col_blocks):
        tile[b, row_blocks] = jnp.zeros((BLOCK, BLOCK), jnp.bfloat16)
    for t in range(STEPS):
        near[t, CAP] = jnp.zeros((HALF, BLOCK), jnp.bfloat16)
        far[t, CAP] = jnp.zeros((HALF, BLOCK), jnp.bfloat16)

    first = jnp.int32(4 * (row_blocks - 1))
    nxt[4 * row_blocks] = first
    for q in reversed(range(4 * row_blocks)):
        a, b = q // 4, q % 4
        if b < col_blocks:
            bit = mask[g * row_blocks + a, j * col_blocks + b]
            first = first + bit * (q - first)
        nxt[q] = first

    for t in range(STEPS):
        at = owner[t, g] * col_blocks
        count = jnp.int32(0)
        for a in range(row_blocks):
            for b in range(col_blocks):
                bit = mask[g * row_blocks + a, at + b]
                slots[t, a * col_blocks + b] = CAP + bit * (count - CAP)
                count = count + bit

    for load in loads:
        load.wait()

    q = nxt[0]
    for s in range(CAP):
        block = tile[q & 3, q >> 2]
        packed[0, s] = block[:HALF]
        packed[1, s] = block[HALF:]
        q = nxt[q + 1]

    for t in range(STEPS):
        slab = (owner[t, lax.rem(g - t + n_col, n_col)] & (sub - 1)) * col_blocks
        for a in range(col_blocks):
            for b in range(col_blocks):
                bit = mask[g * row_blocks + slab + a, j * col_blocks + b]
                line = row_blocks + bit * (slab + a - row_blocks)
                block = tile[b, line]
                if t == 0:
                    r_all[0, a * BLOCK : (a + 1) * BLOCK, b * BLOCK : (b + 1) * BLOCK] = block
                else:
                    r_send[t - 1, a * BLOCK : (a + 1) * BLOCK, b * BLOCK : (b + 1) * BLOCK] = block

    pl.semaphore_wait(barrier, len(senders))

    def remote(src, dst, send, recv, device):
        return pltpu.make_async_remote_copy(
            src_ref=src, dst_ref=dst, send_sem=send, recv_sem=recv, device_id=device, device_id_type=MESH
        )

    def part(k):
        return pl.ds(k * SPAN, SPAN)

    swap = remote(packed.at[1 - core], packed.at[2], swap_s, swap_r, mate)

    def cross(k):
        return remote(chosen.at[part(k)], crossed.at[part(k)], cross_s.at[k], cross_r.at[k], across)

    def ring(t, k, by, sems):
        return remote(near.at[t, part(k)], near.at[t, part(k)], sems.at[t, k], ring_r.at[t, k], at_plane(by))

    def hand(t, k):
        return remote(near.at[t, part(k)], far.at[t, part(k)], mate_s.at[t, k], mate_r.at[t, k], mate)

    slabs = [
        remote(r_send.at[t - 1], r_all.at[t], slab_s.at[t - 1], slab_r.at[t - 1], at_grid_row(-t))
        for t in range(1, STEPS)
    ]

    pick = owner[jnp.minimum(rel, STEPS - 1), g] & (sub - 1)

    @pl.when(is_source)
    def _():
        swap.start()
        swap.wait_recv()
        kept = core + ((pick + core) & 1) * (2 - core)

        @pl.loop(0, CHUNKS)
        def _(k):
            chosen[part(k)] = packed[kept, part(k)]
            cross(k).start()

    for copy in slabs:
        copy.start()

    def up_reach(t):
        return jnp.where(t < 2, 2, 5)

    def down_reach(t):
        return jnp.where(t < 2, 5, 2)

    moved = ((pick >> 1) + place // 2) & 1
    from_across = jnp.full((SPAN, HALF, BLOCK), moved, jnp.int32).astype(jnp.float32).astype(jnp.bfloat16)

    @pl.loop(0, CHUNKS + 5 * LAG + CHUNKS - LAG)
    def _(step):
        @pl.when(is_source & (step < CHUNKS))
        def _():
            cross(step).wait_recv()
            near[rel, part(step)] = chosen[part(step)] * (1 - from_across) + crossed[part(step)] * from_across
            ring(rel, step, 1, up_s).start()
            ring(rel, step, -1, down_s).start()
            hand(rel, step).start()

        for h in range(1, 6):
            for by in (1, -1):
                t = lax.rem(rel - by * h + planes, planes)
                reach = up_reach(t) if by == 1 else down_reach(t)
                lead = STEPS - 1 if by == 1 else 0
                behind = jnp.where(t == lead, 0, 0 if h == 1 else CHUNKS - LAG)
                k = step - LAG * h - behind

                @pl.when((t < STEPS) & (h <= reach) & (k >= 0) & (k < CHUNKS))
                def _():
                    sems = up_s if by == 1 else down_s
                    ring(t, k, by, sems).wait_recv()

                    @pl.when(h < reach)
                    def _():
                        ring(t, k, by, sems).start()

                    hand(t, k).start()

    for copy in slabs:
        copy.wait_recv()

    @pl.loop(0, STEPS * CHUNKS)
    def _(i):
        hand(i // CHUNKS, lax.rem(i, CHUNKS)).wait_recv()

    @pl.loop(0, row_blocks)
    def _(a):
        for t in range(STEPS):
            for b in range(col_blocks):
                slot = slots[t, a * col_blocks + b]
                lanes = slice((t * col_blocks + b) * BLOCK, (t * col_blocks + b + 1) * BLOCK)
                for source, half in ((near, core), (far, 1 - core)):
                    wide[pl.ds(pl.multiple_of(a * BLOCK + half * HALF, HALF), HALF), lanes] = source[t, slot]

    @pl.loop(0, row_blocks // 2)
    def _(i):
        at = pl.ds(pl.multiple_of(i * 2 * BLOCK, 2 * BLOCK), 2 * BLOCK)
        total = jnp.dot(wide[at, :], r_all[...].reshape(STEPS * width, width), preferred_element_type=jnp.float32)
        out[at, :] = total

    @pl.when(is_source)
    def _():
        swap.wait_send()

        @pl.loop(0, CHUNKS)
        def _(k):
            cross(k).wait_send()

    for copy in slabs:
        copy.wait_send()

    @pl.loop(0, STEPS * CHUNKS)
    def _(i):
        t, k = i // CHUNKS, lax.rem(i, CHUNKS)
        hand(t, k).wait_send()

        @pl.when(lax.rem(rel - t + planes, planes) < up_reach(t))
        def _():
            ring(t, k, 1, up_s).wait_send()

        @pl.when(lax.rem(t - rel + planes, planes) < down_reach(t))
        def _():
            ring(t, k, -1, down_s).wait_send()


def shards(density, block_mask, owner):
    rows, width = density.shape
    n_row, n_col = lax.axis_size("row"), lax.axis_size("col")
    dma = pltpu.SemaphoreType.DMA
    bf16 = jnp.bfloat16
    piece = (CAP, HALF, BLOCK)
    return pl.pallas_call(
        functools.partial(kernel, n_row, n_col),
        out_shape=jax.ShapeDtypeStruct((rows, width), jnp.float32),
        in_specs=[
            pl.BlockSpec(memory_space=pl.ANY),
            pl.BlockSpec(memory_space=pltpu.SMEM),
            pl.BlockSpec(memory_space=pltpu.SMEM),
        ],
        out_specs=pl.BlockSpec(memory_space=pltpu.VMEM),
        scratch_shapes=[
            pltpu.VMEM((width // BLOCK, rows // BLOCK + 1, BLOCK, BLOCK), bf16),
            pltpu.SMEM((4 * rows // BLOCK + 1,), jnp.int32),
            pltpu.SMEM((STEPS, rows // BLOCK * (width // BLOCK)), jnp.int32),
            pltpu.VMEM((3, *piece), bf16),
            pltpu.VMEM(piece, bf16),
            pltpu.VMEM(piece, bf16),
            pltpu.VMEM((STEPS, CAP + 1, HALF, BLOCK), bf16),
            pltpu.VMEM((STEPS, CAP + 1, HALF, BLOCK), bf16),
            pltpu.VMEM((STEPS - 1, width, width), bf16),
            pltpu.VMEM((STEPS, width, width), bf16),
            pltpu.VMEM((rows, STEPS * width), bf16),
            dma((width // BLOCK,)), dma, dma, dma((CHUNKS,)), dma((CHUNKS,)),
            dma((STEPS, CHUNKS)), dma((STEPS, CHUNKS)), dma((STEPS, CHUNKS)),
            dma((STEPS, CHUNKS)), dma((STEPS, CHUNKS)),
            dma((STEPS - 1,)), dma((STEPS - 1,)),
        ],
        compiler_params=pltpu.CompilerParams(
            collective_id=0, has_side_effects=True, vmem_limit_bytes=48 * 1024 * 1024
        ),
        cost_estimate=pl.CostEstimate(
            flops=2 * rows * width * width * STEPS, bytes_accessed=rows * width * 6, transcendentals=0
        ),
        name="fox",
    )(density.reshape(rows // BLOCK, BLOCK, width), block_mask, owner)


def solution(mesh):
    placed = (P("col", "row"), P(), P())
    return jax.shard_map(
        shards, mesh=mesh, in_specs=placed, out_specs=P("col", "row"), check_vma=False
    )
```

```python
import functools

import jax
import jax.numpy as jnp
from jax import lax
from jax.experimental import pallas as pl
from jax.experimental.pallas import tpu as pltpu
from jax.sharding import PartitionSpec as P

BLOCK = 128
STEPS = 4
CAP = 21
HALF = BLOCK // 2
CHUNKS = 7
SPAN = CAP // CHUNKS
LAG = 4
SHIFT = 3
DETOUR = 12
READY = 14
UNITS = 6
UP = (3, 3, 4, 4)
MESH = pl.DeviceIdType.MESH


def kernel(
    n_row, n_col, density, mask_in, owner_in, out,
    mask, owner, tile, nxt, slots, packed, swapped, chosen, crossed, held_0, held_1, held_2, held_3, r_send, r_all, passing,
    load_sem, table_sem, swap_s, swap_r, cross_s, cross_r, up_s, down_s, ring_r, mate_s, mate_r, slab_s, slab_r, pass_s, pass_r,
):
    held = (held_0, held_1, held_2, held_3)
    g = lax.axis_index("col")
    j = lax.axis_index("row")
    sub = n_row // n_col
    planes = n_col
    plane = j // sub
    place = lax.rem(j, sub)
    core = lax.rem(place, 2)
    rel = lax.rem(plane - g + planes, planes)
    is_source = rel < STEPS
    row_blocks, _, width = density.shape
    col_blocks = width // BLOCK
    my_rows = pl.ds(pl.multiple_of(core * HALF, HALF), HALF)
    mate_rows = pl.ds(pl.multiple_of((1 - core) * HALF, HALF), HALF)

    def at_plane(by):
        return {"col": g, "row": lax.rem(plane + by + planes, planes) * sub + place}

    def at_grid_row(by):
        return {"col": lax.rem(g + by + n_col, n_col), "row": j}

    mate = {"col": g, "row": plane * sub + place + 1 - 2 * core}
    across = {"col": g, "row": plane * sub + lax.rem(place + 2, sub)}

    barrier = pltpu.get_barrier_semaphore()
    odd = lax.rem(g, 2)
    senders = [mate, across, at_plane(1), at_plane(-1), at_grid_row(1), at_grid_row(2)]
    senders += [at_grid_row(STEPS - 1 - 2 * (STEPS - 1) * odd)]
    for device in senders:
        pl.semaphore_signal(barrier, inc=1, device_id=device, device_id_type=MESH)

    tables = [
        pltpu.make_async_copy(mask_in, mask, table_sem.at[0]),
        pltpu.make_async_copy(owner_in, owner, table_sem.at[1]),
    ]
    loads = [
        pltpu.make_async_copy(
            density.at[:, :, pl.ds(b * BLOCK, BLOCK)], tile.at[b, pl.ds(0, row_blocks)], load_sem.at[b]
        )
        for b in range(col_blocks)
    ]
    for copy in tables + loads:
        copy.start()
    zero = jnp.zeros((BLOCK, BLOCK), jnp.bfloat16)
    for b in range(col_blocks):
        tile[b, row_blocks] = zero
    for t in range(STEPS):
        held[t][CAP] = zero
    for copy in tables:
        copy.wait()

    first = jnp.int32(4 * (row_blocks - 1))
    nxt[4 * row_blocks] = first
    for q in reversed(range(4 * row_blocks)):
        a, b = q // 4, q % 4
        if b < col_blocks:
            bit = mask[g * row_blocks + a, j * col_blocks + b]
            first = first + bit * (q - first)
        nxt[q] = first

    for load in loads:
        load.wait()

    q = nxt[0]
    for s in range(CAP):
        packed[s] = tile[q & 3, q >> 2]
        q = nxt[q + 1]

    @pl.when(odd == 0)
    def _():
        pl.semaphore_signal(barrier, inc=1, device_id=at_grid_row(-2), device_id_type=MESH)

    pl.semaphore_wait(barrier, len(senders) + 1 - odd)

    def remote(src, dst, send, recv, device):
        return pltpu.make_async_remote_copy(
            src_ref=src, dst_ref=dst, send_sem=send, recv_sem=recv, device_id=device, device_id_type=MESH
        )

    def part(k):
        return pl.ds(k * SPAN, SPAN)

    swap = remote(packed.at[:, mate_rows], swapped.at[:], swap_s, swap_r, mate)

    def cross(k):
        return remote(chosen.at[part(k)], crossed.at[part(k)], cross_s.at[k], cross_r.at[k], across)

    def ring(t, k, by, sems):
        span = held[t].at[part(k), my_rows]
        return remote(span, span, sems.at[t, k], ring_r.at[t, k], at_plane(by))

    early = CHUNKS // 2 + 1

    def hand(t, late):
        blocks = pl.ds(early * SPAN, (CHUNKS - early) * SPAN) if late else pl.ds(0, early * SPAN)
        span = held[t].at[blocks, my_rows]
        return remote(span, span, mate_s.at[t, late], mate_r.at[t, late], mate)

    slabs = [
        remote(r_send.at[t - 1], r_all.at[t], slab_s.at[t - 1], slab_r.at[t - 1], at_grid_row(-t))
        for t in range(1, STEPS)
    ]
    detours = lax.rem(g, 2) == 0
    detour = remote(r_send.at[STEPS - 2], passing.at[:], pass_s.at[0], pass_r, at_grid_row(2))
    onto = remote(passing.at[:], r_all.at[STEPS - 1], pass_s.at[1], slab_r.at[STEPS - 2], at_grid_row(STEPS - 1))

    @pl.when(is_source)
    def _():
        swap.start()

    pick = owner[jnp.minimum(rel, STEPS - 1), g] & (sub - 1)

    for t in range(STEPS):
        slab = (owner[t, lax.rem(g - t + n_col, n_col)] & (sub - 1)) * col_blocks
        for a in range(col_blocks):
            for b in range(col_blocks):
                bit = mask[g * row_blocks + slab + a, j * col_blocks + b]
                block = tile[b, row_blocks + bit * (slab + a - row_blocks)]
                if t == 0:
                    r_all[0, a * BLOCK : (a + 1) * BLOCK, b * BLOCK : (b + 1) * BLOCK] = block
                else:
                    r_send[t - 1, a * BLOCK : (a + 1) * BLOCK, b * BLOCK : (b + 1) * BLOCK] = block

    mine = 1 - ((pick + core) & 1)

    def whole(flag):
        return jnp.full((SPAN, HALF, BLOCK), flag, jnp.int32).astype(jnp.float32).astype(jnp.bfloat16)

    @pl.when(is_source)
    def _():
        swap.wait_recv()
        own = whole(mine)

        @pl.loop(0, CHUNKS)
        def _(k):
            chosen[part(k)] = packed[part(k), my_rows] * own + swapped[part(k)] * (1 - own)
            cross(k).start()

    slabs[1].start()
    slabs[0].start()

    @pl.when(detours)
    def _():
        detour.start()

    @pl.when(jnp.logical_not(detours))
    def _():
        slabs[2].start()


    for t in range(STEPS):
        at = owner[t, g] * col_blocks
        count = jnp.int32(0)
        for a in range(row_blocks):
            for b in range(col_blocks):
                bit = mask[g * row_blocks + a, at + b]
                slots[t, a * col_blocks + b] = CAP + bit * (count - CAP)
                count = count + bit
    out[...] = jnp.zeros_like(out)

    moved = whole(((pick >> 1) + place // 2) & 1)

    route = []
    for t in range(STEPS):
        above = lax.rem(rel - t + planes, planes)
        up = above <= UP[t]
        hops = jnp.where(up, above, planes - above)
        nearer = jnp.maximum(jnp.minimum(jnp.where(up, STEPS - 1 - t, t), hops - 1), 0)
        onward = (hops > 0) & (hops < jnp.where(up, UP[t], planes - 1 - UP[t]))
        route.append((up, onward, LAG * hops + SHIFT * nearer))

    unit_rows = row_blocks // UNITS

    @pl.loop(0, LAG * max(UP) + SHIFT * (STEPS - 1) + CHUNKS + 1 + UNITS)
    def _(step):
        @pl.when(is_source & (step < CHUNKS))
        def _():
            cross(step).wait_recv()

        for t in range(STEPS):
            up, onward, begin = route[t]
            k = step - begin

            @pl.when((k >= 0) & (k < CHUNKS))
            def _():
                @pl.when(rel == t)
                def _():
                    held[t][part(k), my_rows] = chosen[part(k)] * (1 - moved) + crossed[part(k)] * moved
                    ring(t, k, 1, up_s).start()
                    ring(t, k, -1, down_s).start()

                @pl.when(rel != t)
                def _():
                    ring(t, k, 1, up_s).wait_recv()

                @pl.when(onward & up)
                def _():
                    ring(t, k, 1, up_s).start()

                @pl.when(onward & jnp.logical_not(up))
                def _():
                    ring(t, k, -1, down_s).start()

                @pl.when(k == early - 1)
                def _():
                    hand(t, 0).start()

                @pl.when(k == CHUNKS - 1)
                def _():
                    hand(t, 1).start()

        @pl.when(detours & (step == DETOUR))
        def _():
            detour.wait_recv()
            onto.start()

        for t in range(STEPS):
            unit = step - jnp.maximum(route[t][2] + CHUNKS + 1, READY + t)

            @pl.when((unit >= 0) & (unit < UNITS))
            def _():
                @pl.when(unit == 0)
                def _():
                    hand(t, 0).wait_recv()
                    hand(t, 1).wait_recv()
                    if t > 0:
                        slabs[t - 1].wait_recv()

                lines = [
                    jnp.concatenate(
                        [
                            held[t][slots[t, (unit * unit_rows + a) * col_blocks + b]]
                            for b in range(col_blocks)
                        ],
                        axis=1,
                    )
                    for a in range(unit_rows)
                ]
                at = pl.ds(pl.multiple_of(unit * unit_rows * BLOCK, unit_rows * BLOCK), unit_rows * BLOCK)
                out[at, :] += jnp.dot(
                    jnp.concatenate(lines, axis=0), r_all[t], preferred_element_type=jnp.float32
                )

    @pl.when(is_source)
    def _():
        swap.wait_send()

        @pl.loop(0, CHUNKS)
        def _(k):
            cross(k).wait_send()

    slabs[0].wait_send()
    slabs[1].wait_send()

    @pl.when(detours)
    def _():
        detour.wait_send()
        onto.wait_send()

    @pl.when(jnp.logical_not(detours))
    def _():
        slabs[2].wait_send()

    for t in range(STEPS):
        up, onward, _ = route[t]
        hand(t, 0).wait_send()
        hand(t, 1).wait_send()

        @pl.when((rel == t) | (onward & up))
        def _():
            @pl.loop(0, CHUNKS)
            def _(k):
                ring(t, k, 1, up_s).wait_send()

        @pl.when((rel == t) | (onward & jnp.logical_not(up)))
        def _():
            @pl.loop(0, CHUNKS)
            def _(k):
                ring(t, k, -1, down_s).wait_send()


def shards(density, block_mask, owner):
    rows, width = density.shape
    row_blocks, col_blocks = rows // BLOCK, width // BLOCK
    n_row, n_col = lax.axis_size("row"), lax.axis_size("col")
    dma = pltpu.SemaphoreType.DMA
    bf16 = jnp.bfloat16
    piece = (CAP, HALF, BLOCK)
    return pl.pallas_call(
        functools.partial(kernel, n_row, n_col),
        out_shape=jax.ShapeDtypeStruct((rows, width), jnp.float32),
        in_specs=[pl.BlockSpec(memory_space=pltpu.HBM)] * 3,
        out_specs=pl.BlockSpec(memory_space=pltpu.VMEM),
        scratch_shapes=[
            pltpu.SMEM(block_mask.shape, jnp.int32),
            pltpu.SMEM(owner.shape, jnp.int32),
            pltpu.VMEM((col_blocks, row_blocks + 1, BLOCK, BLOCK), bf16),
            pltpu.SMEM((4 * row_blocks + 1,), jnp.int32),
            pltpu.SMEM((STEPS, row_blocks * col_blocks), jnp.int32),
            pltpu.VMEM((CAP, BLOCK, BLOCK), bf16),
            pltpu.VMEM(piece, bf16),
            pltpu.VMEM(piece, bf16),
            pltpu.VMEM(piece, bf16),
            *[pltpu.VMEM((CAP + 1, BLOCK, BLOCK), bf16)] * STEPS,
            pltpu.VMEM((STEPS - 1, width, width), bf16),
            pltpu.VMEM((STEPS, width, width), bf16),
            pltpu.VMEM((width, width), bf16),
            dma((col_blocks,)), dma((2,)), dma, dma, dma((CHUNKS,)), dma((CHUNKS,)),
            dma((STEPS, CHUNKS)), dma((STEPS, CHUNKS)), dma((STEPS, CHUNKS)),
            dma((STEPS, 2)), dma((STEPS, 2)),
            dma((STEPS - 1,)), dma((STEPS - 1,)), dma((2,)), dma,
        ],
        compiler_params=pltpu.CompilerParams(
            collective_id=0, has_side_effects=True, vmem_limit_bytes=48 * 1024 * 1024
        ),
        cost_estimate=pl.CostEstimate(
            flops=2 * rows * width * width * STEPS, bytes_accessed=rows * width * 6, transcendentals=0
        ),
        name="fox",
    )(density.reshape(row_blocks, BLOCK, width), block_mask, owner)


def solution(mesh):
    placed = (P("col", "row"), P(), P())
    return jax.shard_map(
        shards, mesh=mesh, in_specs=placed, out_specs=P("col", "row"), check_vma=False
    )
```

```python
import functools

import jax
import jax.numpy as jnp
from jax import lax
from jax.experimental import pallas as pl
from jax.experimental.pallas import tpu as pltpu
from jax.sharding import PartitionSpec as P

BLOCK = 128
STEPS = 4
CAP = 21
HALF = BLOCK // 2
CHUNKS = 7
SPAN = CAP // CHUNKS
LAG = 4
SHIFT = 3
AFTER = 2
DETOUR = 12
READY = 16
UNITS = 4
UP = (3, 3, 4, 4)
MESH = pl.DeviceIdType.MESH


def kernel(
    n_row, n_col, density, mask_in, owner_in, out,
    mask, owner, tile, nxt, slots, packed, swapped, chosen, crossed, held_0, held_1, held_2, held_3, r_send, r_all, passing,
    load_sem, table_sem, swap_s, swap_r, cross_s, cross_r, up_s, down_s, ring_r, mate_s, mate_r, slab_s, slab_r, pass_s, pass_r,
):
    held = (held_0, held_1, held_2, held_3)
    g = lax.axis_index("col")
    j = lax.axis_index("row")
    sub = n_row // n_col
    planes = n_col
    plane = j // sub
    place = lax.rem(j, sub)
    core = lax.rem(place, 2)
    rel = lax.rem(plane - g + planes, planes)
    is_source = rel < STEPS
    row_blocks, _, width = density.shape
    col_blocks = width // BLOCK
    my_rows = pl.ds(pl.multiple_of(core * HALF, HALF), HALF)
    mate_rows = pl.ds(pl.multiple_of((1 - core) * HALF, HALF), HALF)

    def at_plane(by):
        return {"col": g, "row": lax.rem(plane + by + planes, planes) * sub + place}

    def at_grid_row(by):
        return {"col": lax.rem(g + by + n_col, n_col), "row": j}

    mate = {"col": g, "row": plane * sub + place + 1 - 2 * core}
    across = {"col": g, "row": plane * sub + lax.rem(place + 2, sub)}

    barrier = pltpu.get_barrier_semaphore()
    odd = lax.rem(g, 2)
    senders = [mate, across, at_plane(1), at_plane(-1), at_grid_row(1), at_grid_row(2)]
    senders += [at_grid_row(STEPS - 1 - 2 * (STEPS - 1) * odd)]
    for device in senders:
        pl.semaphore_signal(barrier, inc=1, device_id=device, device_id_type=MESH)

    tables = [
        pltpu.make_async_copy(mask_in, mask, table_sem.at[0]),
        pltpu.make_async_copy(owner_in, owner, table_sem.at[1]),
    ]
    loads = [
        pltpu.make_async_copy(
            density.at[:, :, pl.ds(b * BLOCK, BLOCK)], tile.at[b, pl.ds(0, row_blocks)], load_sem.at[b]
        )
        for b in range(col_blocks)
    ]
    for copy in tables + loads:
        copy.start()
    zero = jnp.zeros((BLOCK, BLOCK), jnp.bfloat16)
    for b in range(col_blocks):
        tile[b, row_blocks] = zero
    for t in range(STEPS):
        held[t][CAP] = zero
    for copy in tables:
        copy.wait()

    first = jnp.int32(4 * (row_blocks - 1))
    nxt[4 * row_blocks] = first
    for q in reversed(range(4 * row_blocks)):
        a, b = q // 4, q % 4
        if b < col_blocks:
            bit = mask[g * row_blocks + a, j * col_blocks + b]
            first = first + bit * (q - first)
        nxt[q] = first

    for load in loads:
        load.wait()

    q = nxt[0]
    for s in range(CAP):
        packed[s] = tile[q & 3, q >> 2]
        q = nxt[q + 1]

    @pl.when(odd == 0)
    def _():
        pl.semaphore_signal(barrier, inc=1, device_id=at_grid_row(-2), device_id_type=MESH)

    pl.semaphore_wait(barrier, len(senders) + 1 - odd)

    def remote(src, dst, send, recv, device):
        return pltpu.make_async_remote_copy(
            src_ref=src, dst_ref=dst, send_sem=send, recv_sem=recv, device_id=device, device_id_type=MESH
        )

    def part(k):
        return pl.ds(k * SPAN, SPAN)

    swap = remote(packed.at[:, mate_rows], swapped.at[:], swap_s, swap_r, mate)

    def cross(k):
        return remote(chosen.at[part(k)], crossed.at[part(k)], cross_s.at[k], cross_r.at[k], across)

    def ring(t, k, by, sems):
        span = held[t].at[part(k), my_rows]
        return remote(span, span, sems.at[t, k], ring_r.at[t, k], at_plane(by))

    early = CHUNKS // 2 + 1

    def hand(t, late):
        blocks = pl.ds(early * SPAN, (CHUNKS - early) * SPAN) if late else pl.ds(0, early * SPAN)
        span = held[t].at[blocks, my_rows]
        return remote(span, span, mate_s.at[t, late], mate_r.at[t, late], mate)

    slabs = [
        remote(r_send.at[t - 1], r_all.at[t], slab_s.at[t - 1], slab_r.at[t - 1], at_grid_row(-t))
        for t in range(1, STEPS)
    ]
    detours = lax.rem(g, 2) == 0
    detour = remote(r_send.at[STEPS - 2], passing.at[:], pass_s.at[0], pass_r, at_grid_row(2))
    onto = remote(passing.at[:], r_all.at[STEPS - 1], pass_s.at[1], slab_r.at[STEPS - 2], at_grid_row(STEPS - 1))

    @pl.when(is_source)
    def _():
        swap.start()

    pick = owner[jnp.minimum(rel, STEPS - 1), g] & (sub - 1)

    for t in range(STEPS):
        slab = (owner[t, lax.rem(g - t + n_col, n_col)] & (sub - 1)) * col_blocks
        for a in range(col_blocks):
            for b in range(col_blocks):
                bit = mask[g * row_blocks + slab + a, j * col_blocks + b]
                block = tile[b, row_blocks + bit * (slab + a - row_blocks)]
                if t == 0:
                    r_all[0, a * BLOCK : (a + 1) * BLOCK, b * BLOCK : (b + 1) * BLOCK] = block
                else:
                    r_send[t - 1, a * BLOCK : (a + 1) * BLOCK, b * BLOCK : (b + 1) * BLOCK] = block

    mine = 1 - ((pick + core) & 1)

    def whole(flag):
        return jnp.full((SPAN, HALF, BLOCK), flag, jnp.int32).astype(jnp.float32).astype(jnp.bfloat16)

    @pl.when(is_source)
    def _():
        swap.wait_recv()
        own = whole(mine)

        @pl.loop(0, CHUNKS)
        def _(k):
            chosen[part(k)] = packed[part(k), my_rows] * own + swapped[part(k)] * (1 - own)
            cross(k).start()

    slabs[1].start()
    slabs[0].start()

    @pl.when(detours)
    def _():
        detour.start()

    @pl.when(jnp.logical_not(detours))
    def _():
        slabs[2].start()


    for t in range(STEPS):
        at = owner[t, g] * col_blocks
        count = jnp.int32(0)
        for a in range(row_blocks):
            for b in range(col_blocks):
                bit = mask[g * row_blocks + a, at + b]
                slots[t, a * col_blocks + b] = CAP + bit * (count - CAP)
                count = count + bit
    out[...] = jnp.zeros_like(out)

    moved = whole(((pick >> 1) + place // 2) & 1)

    route = []
    for t in range(STEPS):
        above = lax.rem(rel - t + planes, planes)
        up = above <= UP[t]
        hops = jnp.where(up, above, planes - above)
        nearer = jnp.maximum(jnp.minimum(jnp.where(up, STEPS - 1 - t, t), hops - 1), 0)
        onward = (hops > 0) & (hops < jnp.where(up, UP[t], planes - 1 - UP[t]))
        route.append((up, onward, jnp.where(hops > 0, LAG * hops + SHIFT * nearer + AFTER, 0)))

    unit_rows = row_blocks // UNITS

    @pl.loop(0, LAG * max(UP) + SHIFT * (STEPS - 1) + AFTER + CHUNKS + 1 + UNITS)
    def _(step):
        @pl.when(is_source & (step < CHUNKS))
        def _():
            cross(step).wait_recv()

        for t in range(STEPS):
            up, onward, begin = route[t]
            k = step - begin

            @pl.when((k >= 0) & (k < CHUNKS))
            def _():
                @pl.when(rel == t)
                def _():
                    held[t][part(k), my_rows] = chosen[part(k)] * (1 - moved) + crossed[part(k)] * moved
                    ring(t, k, 1, up_s).start()
                    ring(t, k, -1, down_s).start()

                @pl.when(rel != t)
                def _():
                    ring(t, k, 1, up_s).wait_recv()

                @pl.when(onward & up)
                def _():
                    ring(t, k, 1, up_s).start()

                @pl.when(onward & jnp.logical_not(up))
                def _():
                    ring(t, k, -1, down_s).start()

                @pl.when(k == early - 1)
                def _():
                    hand(t, 0).start()

                @pl.when(k == CHUNKS - 1)
                def _():
                    hand(t, 1).start()

        @pl.when(detours & (step == DETOUR))
        def _():
            detour.wait_recv()
            onto.start()

        for t in range(STEPS):
            unit = step - jnp.maximum(route[t][2] + CHUNKS + 1, READY + t)

            @pl.when((unit >= 0) & (unit < UNITS))
            def _():
                @pl.when(unit == 0)
                def _():
                    hand(t, 0).wait_recv()
                    hand(t, 1).wait_recv()
                    if t > 0:
                        slabs[t - 1].wait_recv()

                lines = [
                    jnp.concatenate(
                        [
                            held[t][slots[t, (unit * unit_rows + a) * col_blocks + b]]
                            for b in range(col_blocks)
                        ],
                        axis=1,
                    )
                    for a in range(unit_rows)
                ]
                at = pl.ds(pl.multiple_of(unit * unit_rows * BLOCK, unit_rows * BLOCK), unit_rows * BLOCK)
                out[at, :] += jnp.dot(
                    jnp.concatenate(lines, axis=0), r_all[t], preferred_element_type=jnp.float32
                )

    @pl.when(is_source)
    def _():
        swap.wait_send()

        @pl.loop(0, CHUNKS)
        def _(k):
            cross(k).wait_send()

    slabs[0].wait_send()
    slabs[1].wait_send()

    @pl.when(detours)
    def _():
        detour.wait_send()
        onto.wait_send()

    @pl.when(jnp.logical_not(detours))
    def _():
        slabs[2].wait_send()

    for t in range(STEPS):
        up, onward, _ = route[t]
        hand(t, 0).wait_send()
        hand(t, 1).wait_send()

        @pl.when((rel == t) | (onward & up))
        def _():
            @pl.loop(0, CHUNKS)
            def _(k):
                ring(t, k, 1, up_s).wait_send()

        @pl.when((rel == t) | (onward & jnp.logical_not(up)))
        def _():
            @pl.loop(0, CHUNKS)
            def _(k):
                ring(t, k, -1, down_s).wait_send()


def shards(density, block_mask, owner):
    rows, width = density.shape
    row_blocks, col_blocks = rows // BLOCK, width // BLOCK
    n_row, n_col = lax.axis_size("row"), lax.axis_size("col")
    dma = pltpu.SemaphoreType.DMA
    bf16 = jnp.bfloat16
    piece = (CAP, HALF, BLOCK)
    return pl.pallas_call(
        functools.partial(kernel, n_row, n_col),
        out_shape=jax.ShapeDtypeStruct((rows, width), jnp.float32),
        in_specs=[pl.BlockSpec(memory_space=pltpu.HBM)] * 3,
        out_specs=pl.BlockSpec(memory_space=pltpu.VMEM),
        scratch_shapes=[
            pltpu.SMEM(block_mask.shape, jnp.int32),
            pltpu.SMEM(owner.shape, jnp.int32),
            pltpu.VMEM((col_blocks, row_blocks + 1, BLOCK, BLOCK), bf16),
            pltpu.SMEM((4 * row_blocks + 1,), jnp.int32),
            pltpu.SMEM((STEPS, row_blocks * col_blocks), jnp.int32),
            pltpu.VMEM((CAP, BLOCK, BLOCK), bf16),
            pltpu.VMEM(piece, bf16),
            pltpu.VMEM(piece, bf16),
            pltpu.VMEM(piece, bf16),
            *[pltpu.VMEM((CAP + 1, BLOCK, BLOCK), bf16)] * STEPS,
            pltpu.VMEM((STEPS - 1, width, width), bf16),
            pltpu.VMEM((STEPS, width, width), bf16),
            pltpu.VMEM((width, width), bf16),
            dma((col_blocks,)), dma((2,)), dma, dma, dma((CHUNKS,)), dma((CHUNKS,)),
            dma((STEPS, CHUNKS)), dma((STEPS, CHUNKS)), dma((STEPS, CHUNKS)),
            dma((STEPS, 2)), dma((STEPS, 2)),
            dma((STEPS - 1,)), dma((STEPS - 1,)), dma((2,)), dma,
        ],
        compiler_params=pltpu.CompilerParams(
            collective_id=0, has_side_effects=True, vmem_limit_bytes=48 * 1024 * 1024
        ),
        cost_estimate=pl.CostEstimate(
            flops=2 * rows * width * width * STEPS, bytes_accessed=rows * width * 6, transcendentals=0
        ),
        name="fox",
    )(density.reshape(row_blocks, BLOCK, width), block_mask, owner)


def solution(mesh):
    placed = (P("col", "row"), P(), P())
    return jax.shard_map(
        shards, mesh=mesh, in_specs=placed, out_specs=P("col", "row"), check_vma=False
    )
```

```python
import functools

import jax
import jax.numpy as jnp
from jax import lax
from jax.experimental import pallas as pl
from jax.experimental.pallas import tpu as pltpu
from jax.sharding import PartitionSpec as P

BLOCK = 128
STEPS = 4
CAP = 21
HALF = BLOCK // 2
CHUNKS = 7
SPAN = CAP // CHUNKS
LAG = 4
SHIFT = 3
AFTER = 2
DETOUR = 12
READY = 17
UNITS = 4
UP = (3, 3, 4, 4)
MESH = pl.DeviceIdType.MESH


def kernel(
    n_row, n_col, density, table_in, result,
    table, tile, nxt, slots, packed, swapped, chosen, crossed, near_0, near_1, near_2, near_3, far_0, far_1, far_2, far_3, r_send, r_all, passing, out,
    load_sem, table_sem, swap_s, swap_r, cross_s, cross_r, up_s, down_s, ring_r, mate_s, mate_r, slab_s, slab_r, pass_s, pass_r, out_sem,
):
    near, far = (near_0, near_1, near_2, near_3), (far_0, far_1, far_2, far_3)
    g = lax.axis_index("col")
    j = lax.axis_index("row")
    sub = n_row // n_col
    planes = n_col
    plane = j // sub
    place = lax.rem(j, sub)
    core = lax.rem(place, 2)
    rel = lax.rem(plane - g + planes, planes)
    is_source = rel < STEPS
    row_blocks, _, width = density.shape
    len_mask = n_col * row_blocks
    col_blocks = width // BLOCK
    my_rows = pl.ds(pl.multiple_of(core * HALF, HALF), HALF)
    mate_rows = pl.ds(pl.multiple_of((1 - core) * HALF, HALF), HALF)

    def at_plane(by):
        return {"col": g, "row": lax.rem(plane + by + planes, planes) * sub + place}

    def at_grid_row(by):
        return {"col": lax.rem(g + by + n_col, n_col), "row": j}

    mate = {"col": g, "row": plane * sub + place + 1 - 2 * core}
    across = {"col": g, "row": plane * sub + lax.rem(place + 2, sub)}

    barrier = pltpu.get_barrier_semaphore()
    odd = lax.rem(g, 2)
    senders = [mate, across, at_plane(1), at_plane(-1), at_grid_row(1), at_grid_row(2)]
    senders += [at_grid_row(STEPS - 1 - 2 * (STEPS - 1) * odd)]
    for device in senders:
        pl.semaphore_signal(barrier, inc=1, device_id=device, device_id_type=MESH)

    tables = [pltpu.make_async_copy(table_in, table, table_sem.at[0])]
    loads = [
        pltpu.make_async_copy(
            density.at[:, :, pl.ds(b * BLOCK, BLOCK)], tile.at[b, pl.ds(0, row_blocks)], load_sem.at[b]
        )
        for b in range(col_blocks)
    ]
    for copy in tables + loads:
        copy.start()
    zero = jnp.zeros((BLOCK, BLOCK), jnp.bfloat16)
    for b in range(col_blocks):
        tile[b, row_blocks] = zero
    for t in range(STEPS):
        near[t][CAP] = zero[:HALF]
        far[t][CAP] = zero[:HALF]
    for copy in tables:
        copy.wait()

    first = jnp.int32(4 * (row_blocks - 1))
    nxt[4 * row_blocks] = first
    for q in reversed(range(4 * row_blocks)):
        a, b = q // 4, q % 4
        if b < col_blocks:
            bit = table[g * row_blocks + a, j * col_blocks + b]
            first = first + bit * (q - first)
        nxt[q] = first

    for load in loads:
        load.wait()

    q = nxt[0]
    for s in range(SPAN):
        packed[s] = tile[q & 3, q >> 2]
        q = nxt[q + 1]

    @pl.when(odd == 0)
    def _():
        pl.semaphore_signal(barrier, inc=1, device_id=at_grid_row(-2), device_id_type=MESH)

    pl.semaphore_wait(barrier, len(senders) + 1 - odd)

    def remote(src, dst, send, recv, device):
        return pltpu.make_async_remote_copy(
            src_ref=src, dst_ref=dst, send_sem=send, recv_sem=recv, device_id=device, device_id_type=MESH
        )

    def part(k):
        return pl.ds(k * SPAN, SPAN)

    def swap(n):
        blocks = pl.ds(0, SPAN) if n == 0 else pl.ds(SPAN, CAP - SPAN)
        return remote(packed.at[blocks, mate_rows], swapped.at[blocks], swap_s.at[n], swap_r.at[n], mate)

    def cross(k):
        return remote(chosen.at[part(k)], crossed.at[part(k)], cross_s.at[k], cross_r.at[k], across)

    def ring(t, k, by, sems):
        span = near[t].at[part(k)]
        return remote(span, span, sems.at[t, k], ring_r.at[t, k], at_plane(by))

    early = CHUNKS - 2

    def hand(t, late):
        blocks = pl.ds(early * SPAN, (CHUNKS - early) * SPAN) if late else pl.ds(0, early * SPAN)
        return remote(near[t].at[blocks], far[t].at[blocks], mate_s.at[t, late], mate_r.at[t, late], mate)

    slabs = [
        remote(r_send.at[t - 1], r_all.at[t], slab_s.at[t - 1], slab_r.at[t - 1], at_grid_row(-t))
        for t in range(1, STEPS)
    ]
    detours = lax.rem(g, 2) == 0
    detour = remote(r_send.at[STEPS - 2], passing.at[:], pass_s.at[0], pass_r, at_grid_row(2))
    onto = remote(passing.at[:], r_all.at[STEPS - 1], pass_s.at[1], slab_r.at[STEPS - 2], at_grid_row(STEPS - 1))

    @pl.when(is_source)
    def _():
        swap(0).start()

    for s in range(SPAN, CAP):
        packed[s] = tile[q & 3, q >> 2]
        q = nxt[q + 1]

    @pl.when(is_source)
    def _():
        swap(1).start()

    pick = table[len_mask + jnp.minimum(rel, STEPS - 1), g] & (sub - 1)

    for t in range(STEPS):
        slab = (table[len_mask + t, lax.rem(g - t + n_col, n_col)] & (sub - 1)) * col_blocks
        for a in range(col_blocks):
            for b in range(col_blocks):
                bit = table[g * row_blocks + slab + a, j * col_blocks + b]
                block = tile[b, row_blocks + bit * (slab + a - row_blocks)]
                if t == 0:
                    r_all[0, a * BLOCK : (a + 1) * BLOCK, b * BLOCK : (b + 1) * BLOCK] = block
                else:
                    r_send[t - 1, a * BLOCK : (a + 1) * BLOCK, b * BLOCK : (b + 1) * BLOCK] = block

    mine = 1 - ((pick + core) & 1)

    def whole(flag):
        return jnp.full((SPAN, HALF, BLOCK), flag, jnp.int32).astype(jnp.float32).astype(jnp.bfloat16)

    @pl.when(is_source)
    def _():
        swap(0).wait_recv()
        own = whole(mine)

        @pl.loop(0, CHUNKS)
        def _(k):
            @pl.when(k == 1)
            def _():
                swap(1).wait_recv()

            chosen[part(k)] = packed[part(k), my_rows] * own + swapped[part(k)] * (1 - own)
            cross(k).start()

    slabs[1].start()
    slabs[0].start()

    @pl.when(detours)
    def _():
        detour.start()

    @pl.when(jnp.logical_not(detours))
    def _():
        slabs[2].start()


    for t in range(STEPS):
        at = table[len_mask + t, g] * col_blocks
        count = jnp.int32(0)
        for a in range(row_blocks):
            for b in range(col_blocks):
                bit = table[g * row_blocks + a, at + b]
                slots[t, a * col_blocks + b] = CAP + bit * (count - CAP)
                count = count + bit
    out[...] = jnp.zeros_like(out)

    moved = whole(((pick >> 1) + place // 2) & 1)

    route = []
    for t in range(STEPS):
        above = lax.rem(rel - t + planes, planes)
        up = above <= UP[t]
        hops = jnp.where(up, above, planes - above)
        nearer = jnp.maximum(jnp.minimum(jnp.where(up, STEPS - 1 - t, t), hops - 1), 0)
        onward = (hops > 0) & (hops < jnp.where(up, UP[t], planes - 1 - UP[t]))
        route.append((up, onward, jnp.where(hops > 0, LAG * hops + SHIFT * nearer + AFTER, 0)))

    unit_rows = 2 * row_blocks // UNITS
    starts = [jnp.maximum(begin + CHUNKS, READY + t) for t, (_, _, begin) in enumerate(route)]
    ends = functools.reduce(jnp.maximum, [2 * STEPS * start + t for t, start in enumerate(starts)])

    def place_of(unit):
        half = lax.rem(core + unit // (UNITS // 2), 2)
        first_row = lax.rem(unit, UNITS // 2) * unit_rows
        return first_row, pl.ds(pl.multiple_of(half * HALF, HALF), HALF)

    def finished(unit):
        first_row, lines = place_of(unit)
        at = pl.ds(first_row, unit_rows)
        return pltpu.make_async_copy(out.at[at, lines], result.at[at, lines], out_sem.at[unit])


    @pl.loop(0, LAG * max(UP) + SHIFT * (STEPS - 1) + AFTER + CHUNKS + 1 + UNITS)
    def _(step):
        @pl.when(is_source & (step < CHUNKS))
        def _():
            cross(step).wait_recv()

        for t in range(STEPS):
            up, onward, begin = route[t]
            k = step - begin

            @pl.when((k >= 0) & (k < CHUNKS))
            def _():
                @pl.when(rel == t)
                def _():
                    near[t][part(k)] = chosen[part(k)] * (1 - moved) + crossed[part(k)] * moved
                    ring(t, k, 1, up_s).start()
                    ring(t, k, -1, down_s).start()

                @pl.when(rel != t)
                def _():
                    ring(t, k, 1, up_s).wait_recv()

                @pl.when(onward & up)
                def _():
                    ring(t, k, 1, up_s).start()

                @pl.when(onward & jnp.logical_not(up))
                def _():
                    ring(t, k, -1, down_s).start()

                @pl.when(k == early - 1)
                def _():
                    hand(t, 0).start()

                @pl.when(k == CHUNKS - 1)
                def _():
                    hand(t, 1).start()

        @pl.when(detours & (step == DETOUR))
        def _():
            detour.wait_recv()
            onto.start()

        for t in range(STEPS):
            unit = step - starts[t]

            @pl.when((unit >= 0) & (unit < UNITS))
            def _():
                @pl.when(unit == 0)
                def _():
                    if t > 0:
                        slabs[t - 1].wait_recv()

                @pl.when(unit == UNITS // 2)
                def _():
                    hand(t, 0).wait_recv()
                    hand(t, 1).wait_recv()

                first_row, lines = place_of(unit)
                for rows_of, chosen_half in ((near[t], unit < UNITS // 2), (far[t], unit >= UNITS // 2)):

                    @pl.when(chosen_half)
                    def _():
                        left = [
                            jnp.concatenate(
                                [rows_of[slots[t, (first_row + a) * col_blocks + b]] for b in range(col_blocks)],
                                axis=1,
                            )
                            for a in range(unit_rows)
                        ]
                        product = jnp.dot(
                            jnp.concatenate(left, axis=0), r_all[t], preferred_element_type=jnp.float32
                        )
                        out[pl.ds(first_row, unit_rows), lines] += product.reshape(unit_rows, HALF, width)

                @pl.when(ends == 2 * STEPS * starts[t] + t)
                def _():
                    finished(unit).start()

    @pl.when(is_source)
    def _():
        swap(0).wait_send()
        swap(1).wait_send()

        @pl.loop(0, CHUNKS)
        def _(k):
            cross(k).wait_send()

    for unit in range(UNITS):
        finished(unit).wait()

    slabs[0].wait_send()
    slabs[1].wait_send()

    @pl.when(detours)
    def _():
        detour.wait_send()
        onto.wait_send()

    @pl.when(jnp.logical_not(detours))
    def _():
        slabs[2].wait_send()

    for t in range(STEPS):
        up, onward, _ = route[t]
        hand(t, 0).wait_send()
        hand(t, 1).wait_send()

        @pl.when((rel == t) | (onward & up))
        def _():
            @pl.loop(0, CHUNKS)
            def _(k):
                ring(t, k, 1, up_s).wait_send()

        @pl.when((rel == t) | (onward & jnp.logical_not(up)))
        def _():
            @pl.loop(0, CHUNKS)
            def _(k):
                ring(t, k, -1, down_s).wait_send()


def shards(density, block_mask, owner):
    rows, width = density.shape
    row_blocks, col_blocks = rows // BLOCK, width // BLOCK
    n_row, n_col = lax.axis_size("row"), lax.axis_size("col")
    dma = pltpu.SemaphoreType.DMA
    bf16 = jnp.bfloat16
    piece = (CAP, HALF, BLOCK)
    wide_owner = jnp.pad(owner, ((0, 8 - owner.shape[0]), (0, block_mask.shape[1] - owner.shape[1])))
    table = jnp.concatenate([block_mask, wide_owner], axis=0)
    return pl.pallas_call(
        functools.partial(kernel, n_row, n_col),
        out_shape=jax.ShapeDtypeStruct((row_blocks, BLOCK, width), jnp.float32),
        in_specs=[pl.BlockSpec(memory_space=pltpu.HBM)] * 2,
        out_specs=pl.BlockSpec(memory_space=pl.ANY),
        scratch_shapes=[
            pltpu.SMEM(table.shape, jnp.int32),
            pltpu.VMEM((col_blocks, row_blocks + 1, BLOCK, BLOCK), bf16),
            pltpu.SMEM((4 * row_blocks + 1,), jnp.int32),
            pltpu.SMEM((STEPS, row_blocks * col_blocks), jnp.int32),
            pltpu.VMEM((CAP, BLOCK, BLOCK), bf16),
            pltpu.VMEM(piece, bf16),
            pltpu.VMEM(piece, bf16),
            pltpu.VMEM(piece, bf16),
            *[pltpu.VMEM((CAP + 1, HALF, BLOCK), bf16)] * (2 * STEPS),
            pltpu.VMEM((STEPS - 1, width, width), bf16),
            pltpu.VMEM((STEPS, width, width), bf16),
            pltpu.VMEM((width, width), bf16),
            pltpu.VMEM((row_blocks, BLOCK, width), jnp.float32),
            dma((col_blocks,)), dma((2,)), dma((2,)), dma((2,)), dma((CHUNKS,)), dma((CHUNKS,)),
            dma((STEPS, CHUNKS)), dma((STEPS, CHUNKS)), dma((STEPS, CHUNKS)),
            dma((STEPS, 2)), dma((STEPS, 2)),
            dma((STEPS - 1,)), dma((STEPS - 1,)), dma((2,)), dma, dma((UNITS,)),
        ],
        compiler_params=pltpu.CompilerParams(
            collective_id=0, has_side_effects=True, vmem_limit_bytes=48 * 1024 * 1024
        ),
        cost_estimate=pl.CostEstimate(
            flops=2 * rows * width * width * STEPS, bytes_accessed=rows * width * 6, transcendentals=0
        ),
        name="fox",
    )(density.reshape(row_blocks, BLOCK, width), table).reshape(rows, width)


def solution(mesh):
    placed = (P("col", "row"), P(), P())
    return jax.shard_map(
        shards, mesh=mesh, in_specs=placed, out_specs=P("col", "row"), check_vma=False
    )
```

```python
import functools

import jax
import jax.numpy as jnp
from jax import lax
from jax.experimental import pallas as pl
from jax.experimental.pallas import tpu as pltpu
from jax.sharding import PartitionSpec as P

BLOCK = 128
STEPS = 4
CAP = 21
HALF = BLOCK // 2
CHUNKS = 7
SPAN = CAP // CHUNKS
LAG = 4
SHIFT = 3
AFTER = 2
DETOUR = 12
READY = 17
UNITS = 4
UP = (3, 3, 4, 4)
MESH = pl.DeviceIdType.MESH


def kernel(
    n_row, n_col, density, mask_in, owner_in, result,
    mask, owner, tile, nxt, slots, packed, swapped, chosen, crossed, near_0, near_1, near_2, near_3, far_0, far_1, far_2, far_3, r_send, r_all, passing, out,
    load_sem, table_sem, swap_s, swap_r, cross_s, cross_r, up_s, down_s, ring_r, mate_s, mate_r, slab_s, slab_r, pass_s, pass_r, out_sem,
):
    near, far = (near_0, near_1, near_2, near_3), (far_0, far_1, far_2, far_3)
    g = lax.axis_index("col")
    j = lax.axis_index("row")
    sub = n_row // n_col
    planes = n_col
    plane = j // sub
    place = lax.rem(j, sub)
    core = lax.rem(place, 2)
    rel = lax.rem(plane - g + planes, planes)
    is_source = rel < STEPS
    row_blocks, _, width = density.shape
    col_blocks = width // BLOCK
    my_rows = pl.ds(pl.multiple_of(core * HALF, HALF), HALF)
    mate_rows = pl.ds(pl.multiple_of((1 - core) * HALF, HALF), HALF)

    def at_plane(by):
        return {"col": g, "row": lax.rem(plane + by + planes, planes) * sub + place}

    def at_grid_row(by):
        return {"col": lax.rem(g + by + n_col, n_col), "row": j}

    mate = {"col": g, "row": plane * sub + place + 1 - 2 * core}
    across = {"col": g, "row": plane * sub + lax.rem(place + 2, sub)}

    barrier = pltpu.get_barrier_semaphore()
    odd = lax.rem(g, 2)
    senders = [mate, across, at_plane(1), at_plane(-1), at_grid_row(1), at_grid_row(2)]
    senders += [at_grid_row(STEPS - 1 - 2 * (STEPS - 1) * odd)]
    for device in senders:
        pl.semaphore_signal(barrier, inc=1, device_id=device, device_id_type=MESH)

    tables = [
        pltpu.make_async_copy(mask_in, mask, table_sem.at[0]),
        pltpu.make_async_copy(owner_in, owner, table_sem.at[1]),
    ]
    loads = [
        pltpu.make_async_copy(
            density.at[:, :, pl.ds(b * BLOCK, BLOCK)], tile.at[b, pl.ds(0, row_blocks)], load_sem.at[b]
        )
        for b in range(col_blocks)
    ]
    for copy in tables + loads:
        copy.start()
    zero = jnp.zeros((BLOCK, BLOCK), jnp.bfloat16)
    for b in range(col_blocks):
        tile[b, row_blocks] = zero
    for t in range(STEPS):
        near[t][CAP] = zero[:HALF]
        far[t][CAP] = zero[:HALF]
    for copy in tables:
        copy.wait()

    first = jnp.int32(4 * (row_blocks - 1))
    nxt[4 * row_blocks] = first
    for q in reversed(range(4 * row_blocks)):
        a, b = q // 4, q % 4
        if b < col_blocks:
            bit = mask[g * row_blocks + a, j * col_blocks + b]
            first = first + bit * (q - first)
        nxt[q] = first

    for load in loads:
        load.wait()

    q = nxt[0]
    for s in range(SPAN):
        packed[s] = tile[q & 3, q >> 2]
        q = nxt[q + 1]

    @pl.when(odd == 0)
    def _():
        pl.semaphore_signal(barrier, inc=1, device_id=at_grid_row(-2), device_id_type=MESH)

    pl.semaphore_wait(barrier, len(senders) + 1 - odd)

    def remote(src, dst, send, recv, device):
        return pltpu.make_async_remote_copy(
            src_ref=src, dst_ref=dst, send_sem=send, recv_sem=recv, device_id=device, device_id_type=MESH
        )

    def part(k):
        return pl.ds(k * SPAN, SPAN)

    def swap(n):
        blocks = pl.ds(0, SPAN) if n == 0 else pl.ds(SPAN, CAP - SPAN)
        return remote(packed.at[blocks, mate_rows], swapped.at[blocks], swap_s.at[n], swap_r.at[n], mate)

    def cross(k):
        return remote(chosen.at[part(k)], crossed.at[part(k)], cross_s.at[k], cross_r.at[k], across)

    def ring(t, k, by, sems):
        span = near[t].at[part(k)]
        return remote(span, span, sems.at[t, k], ring_r.at[t, k], at_plane(by))

    early = CHUNKS - 2

    def hand(t, late):
        blocks = pl.ds(early * SPAN, (CHUNKS - early) * SPAN) if late else pl.ds(0, early * SPAN)
        return remote(near[t].at[blocks], far[t].at[blocks], mate_s.at[t, late], mate_r.at[t, late], mate)

    slabs = [
        remote(r_send.at[t - 1], r_all.at[t], slab_s.at[t - 1], slab_r.at[t - 1], at_grid_row(-t))
        for t in range(1, STEPS)
    ]
    detours = lax.rem(g, 2) == 0
    detour = remote(r_send.at[STEPS - 2], passing.at[:], pass_s.at[0], pass_r, at_grid_row(2))
    onto = remote(passing.at[:], r_all.at[STEPS - 1], pass_s.at[1], slab_r.at[STEPS - 2], at_grid_row(STEPS - 1))

    @pl.when(is_source)
    def _():
        swap(0).start()

    for s in range(SPAN, CAP):
        packed[s] = tile[q & 3, q >> 2]
        q = nxt[q + 1]

    @pl.when(is_source)
    def _():
        swap(1).start()

    pick = owner[jnp.minimum(rel, STEPS - 1), g] & (sub - 1)

    for t in range(STEPS):
        slab = (owner[t, lax.rem(g - t + n_col, n_col)] & (sub - 1)) * col_blocks
        for a in range(col_blocks):
            for b in range(col_blocks):
                bit = mask[g * row_blocks + slab + a, j * col_blocks + b]
                block = tile[b, row_blocks + bit * (slab + a - row_blocks)]
                if t == 0:
                    r_all[0, a * BLOCK : (a + 1) * BLOCK, b * BLOCK : (b + 1) * BLOCK] = block
                else:
                    r_send[t - 1, a * BLOCK : (a + 1) * BLOCK, b * BLOCK : (b + 1) * BLOCK] = block

    mine = 1 - ((pick + core) & 1)

    def whole(flag):
        return jnp.full((SPAN, HALF, BLOCK), flag, jnp.int32).astype(jnp.float32).astype(jnp.bfloat16)

    @pl.when(is_source)
    def _():
        swap(0).wait_recv()
        own = whole(mine)

        @pl.loop(0, CHUNKS)
        def _(k):
            @pl.when(k == 1)
            def _():
                swap(1).wait_recv()

            chosen[part(k)] = packed[part(k), my_rows] * own + swapped[part(k)] * (1 - own)
            cross(k).start()

    slabs[1].start()
    slabs[0].start()

    @pl.when(detours)
    def _():
        detour.start()

    @pl.when(jnp.logical_not(detours))
    def _():
        slabs[2].start()


    for t in range(STEPS):
        at = owner[t, g] * col_blocks
        count = jnp.int32(0)
        for a in range(row_blocks):
            for b in range(col_blocks):
                bit = mask[g * row_blocks + a, at + b]
                slots[t, a * col_blocks + b] = CAP + bit * (count - CAP)
                count = count + bit
    out[...] = jnp.zeros_like(out)

    moved = whole(((pick >> 1) + place // 2) & 1)

    route = []
    for t in range(STEPS):
        above = lax.rem(rel - t + planes, planes)
        up = above <= UP[t]
        hops = jnp.where(up, above, planes - above)
        nearer = jnp.maximum(jnp.minimum(jnp.where(up, STEPS - 1 - t, t), hops - 1), 0)
        onward = (hops > 0) & (hops < jnp.where(up, UP[t], planes - 1 - UP[t]))
        route.append((up, onward, jnp.where(hops > 0, LAG * hops + SHIFT * nearer + AFTER, 0)))

    unit_rows = 2 * row_blocks // UNITS
    starts = [jnp.maximum(begin + CHUNKS, READY + t) for t, (_, _, begin) in enumerate(route)]
    ends = functools.reduce(jnp.maximum, [2 * STEPS * start + t for t, start in enumerate(starts)])

    def place_of(unit):
        half = lax.rem(core + unit // (UNITS // 2), 2)
        first_row = lax.rem(unit, UNITS // 2) * unit_rows
        return first_row, pl.ds(pl.multiple_of(half * HALF, HALF), HALF)

    def finished(unit):
        first_row, lines = place_of(unit)
        at = pl.ds(first_row, unit_rows)
        return pltpu.make_async_copy(out.at[at, lines], result.at[at, lines], out_sem.at[unit])


    @pl.loop(0, LAG * max(UP) + SHIFT * (STEPS - 1) + AFTER + CHUNKS + 1 + UNITS)
    def _(step):
        @pl.when(is_source & (step < CHUNKS))
        def _():
            cross(step).wait_recv()

        for t in range(STEPS):
            up, onward, begin = route[t]
            k = step - begin

            @pl.when((k >= 0) & (k < CHUNKS))
            def _():
                @pl.when(rel == t)
                def _():
                    near[t][part(k)] = chosen[part(k)] * (1 - moved) + crossed[part(k)] * moved
                    ring(t, k, 1, up_s).start()
                    ring(t, k, -1, down_s).start()

                @pl.when(rel != t)
                def _():
                    ring(t, k, 1, up_s).wait_recv()

                @pl.when(onward & up)
                def _():
                    ring(t, k, 1, up_s).start()

                @pl.when(onward & jnp.logical_not(up))
                def _():
                    ring(t, k, -1, down_s).start()

                @pl.when(k == early - 1)
                def _():
                    hand(t, 0).start()

                @pl.when(k == CHUNKS - 1)
                def _():
                    hand(t, 1).start()

        @pl.when(detours & (step == DETOUR))
        def _():
            detour.wait_recv()
            onto.start()

        for t in range(STEPS):
            unit = step - starts[t]

            @pl.when((unit >= 0) & (unit < UNITS))
            def _():
                @pl.when(unit == 0)
                def _():
                    if t > 0:
                        slabs[t - 1].wait_recv()

                @pl.when(unit == UNITS // 2)
                def _():
                    hand(t, 0).wait_recv()
                    hand(t, 1).wait_recv()

                first_row, lines = place_of(unit)
                for rows_of, chosen_half in ((near[t], unit < UNITS // 2), (far[t], unit >= UNITS // 2)):

                    @pl.when(chosen_half)
                    def _():
                        left = [
                            jnp.concatenate(
                                [rows_of[slots[t, (first_row + a) * col_blocks + b]] for b in range(col_blocks)],
                                axis=1,
                            )
                            for a in range(unit_rows)
                        ]
                        product = jnp.dot(
                            jnp.concatenate(left, axis=0), r_all[t], preferred_element_type=jnp.float32
                        )
                        out[pl.ds(first_row, unit_rows), lines] += product.reshape(unit_rows, HALF, width)

                @pl.when(ends == 2 * STEPS * starts[t] + t)
                def _():
                    finished(unit).start()

    @pl.when(is_source)
    def _():
        swap(0).wait_send()
        swap(1).wait_send()

        @pl.loop(0, CHUNKS)
        def _(k):
            cross(k).wait_send()

    for unit in range(UNITS):
        finished(unit).wait()

    slabs[0].wait_send()
    slabs[1].wait_send()

    @pl.when(detours)
    def _():
        detour.wait_send()
        onto.wait_send()

    @pl.when(jnp.logical_not(detours))
    def _():
        slabs[2].wait_send()

    for t in range(STEPS):
        up, onward, _ = route[t]
        hand(t, 0).wait_send()
        hand(t, 1).wait_send()

        @pl.when((rel == t) | (onward & up))
        def _():
            @pl.loop(0, CHUNKS)
            def _(k):
                ring(t, k, 1, up_s).wait_send()

        @pl.when((rel == t) | (onward & jnp.logical_not(up)))
        def _():
            @pl.loop(0, CHUNKS)
            def _(k):
                ring(t, k, -1, down_s).wait_send()


def shards(density, block_mask, owner):
    rows, width = density.shape
    row_blocks, col_blocks = rows // BLOCK, width // BLOCK
    n_row, n_col = lax.axis_size("row"), lax.axis_size("col")
    dma = pltpu.SemaphoreType.DMA
    bf16 = jnp.bfloat16
    piece = (CAP, HALF, BLOCK)
    operands = [
        pltpu.with_memory_space_constraint(operand, pltpu.HBM)
        for operand in (density.reshape(row_blocks, BLOCK, width), block_mask, owner)
    ]
    return pl.pallas_call(
        functools.partial(kernel, n_row, n_col),
        out_shape=jax.ShapeDtypeStruct((row_blocks, BLOCK, width), jnp.float32),
        in_specs=[pl.BlockSpec(memory_space=pltpu.HBM)] * 3,
        out_specs=pl.BlockSpec(memory_space=pl.ANY),
        scratch_shapes=[
            pltpu.SMEM(block_mask.shape, jnp.int32),
            pltpu.SMEM(owner.shape, jnp.int32),
            pltpu.VMEM((col_blocks, row_blocks + 1, BLOCK, BLOCK), bf16),
            pltpu.SMEM((4 * row_blocks + 1,), jnp.int32),
            pltpu.SMEM((STEPS, row_blocks * col_blocks), jnp.int32),
            pltpu.VMEM((CAP, BLOCK, BLOCK), bf16),
            pltpu.VMEM(piece, bf16),
            pltpu.VMEM(piece, bf16),
            pltpu.VMEM(piece, bf16),
            *[pltpu.VMEM((CAP + 1, HALF, BLOCK), bf16)] * (2 * STEPS),
            pltpu.VMEM((STEPS - 1, width, width), bf16),
            pltpu.VMEM((STEPS, width, width), bf16),
            pltpu.VMEM((width, width), bf16),
            pltpu.VMEM((row_blocks, BLOCK, width), jnp.float32),
            dma((col_blocks,)), dma((2,)), dma((2,)), dma((2,)), dma((CHUNKS,)), dma((CHUNKS,)),
            dma((STEPS, CHUNKS)), dma((STEPS, CHUNKS)), dma((STEPS, CHUNKS)),
            dma((STEPS, 2)), dma((STEPS, 2)),
            dma((STEPS - 1,)), dma((STEPS - 1,)), dma((2,)), dma, dma((UNITS,)),
        ],
        compiler_params=pltpu.CompilerParams(
            collective_id=0, has_side_effects=True, vmem_limit_bytes=48 * 1024 * 1024
        ),
        cost_estimate=pl.CostEstimate(
            flops=2 * rows * width * width * STEPS, bytes_accessed=rows * width * 6, transcendentals=0
        ),
        name="fox",
    )(*operands).reshape(rows, width)


def solution(mesh):
    placed = (P("col", "row"), P(), P())
    return jax.shard_map(
        shards, mesh=mesh, in_specs=placed, out_specs=P("col", "row"), check_vma=False
    )
```

```python
import functools

import jax
import jax.numpy as jnp
from jax import lax
from jax.experimental import pallas as pl
from jax.experimental.pallas import tpu as pltpu
from jax.sharding import PartitionSpec as P

BLOCK = 128
STEPS = 4
CAP = 21
HALF = BLOCK // 2
CHUNKS = 7
SPAN = CAP // CHUNKS
LAG = 4
SHIFT = 4
AFTER = 2
DETOUR = 12
READY = 17
UNITS = 4
UP = (3, 3, 4, 4)
MESH = pl.DeviceIdType.MESH


def kernel(
    n_row, n_col, density, mask_in, owner_in, result,
    mask, owner, tile, nxt, slots, packed, swapped, chosen, crossed, near_0, near_1, near_2, near_3, far_0, far_1, far_2, far_3, r_send, r_all, passing, out,
    load_sem, table_sem, swap_s, swap_r, cross_s, cross_r, up_s, down_s, ring_r, mate_s, mate_r, slab_s, slab_r, pass_s, pass_r, out_sem,
):
    near, far = (near_0, near_1, near_2, near_3), (far_0, far_1, far_2, far_3)
    g = lax.axis_index("col")
    j = lax.axis_index("row")
    sub = n_row // n_col
    planes = n_col
    plane = j // sub
    place = lax.rem(j, sub)
    core = lax.rem(place, 2)
    rel = lax.rem(plane - g + planes, planes)
    is_source = rel < STEPS
    row_blocks, _, width = density.shape
    col_blocks = width // BLOCK
    my_rows = pl.ds(pl.multiple_of(core * HALF, HALF), HALF)
    mate_rows = pl.ds(pl.multiple_of((1 - core) * HALF, HALF), HALF)

    def at_plane(by):
        return {"col": g, "row": lax.rem(plane + by + planes, planes) * sub + place}

    def at_grid_row(by):
        return {"col": lax.rem(g + by + n_col, n_col), "row": j}

    mate = {"col": g, "row": plane * sub + place + 1 - 2 * core}
    across = {"col": g, "row": plane * sub + lax.rem(place + 2, sub)}

    barrier = pltpu.get_barrier_semaphore()
    odd = lax.rem(g, 2)
    senders = [mate, across, at_plane(1), at_plane(-1), at_grid_row(1), at_grid_row(2)]
    senders += [at_grid_row(STEPS - 1 - 2 * (STEPS - 1) * odd)]
    for device in senders:
        pl.semaphore_signal(barrier, inc=1, device_id=device, device_id_type=MESH)

    tables = [
        pltpu.make_async_copy(mask_in, mask, table_sem.at[0]),
        pltpu.make_async_copy(owner_in, owner, table_sem.at[1]),
    ]
    loads = [
        pltpu.make_async_copy(
            density.at[:, :, pl.ds(b * BLOCK, BLOCK)], tile.at[b, pl.ds(0, row_blocks)], load_sem.at[b]
        )
        for b in range(col_blocks)
    ]
    for copy in tables + loads:
        copy.start()
    zero = jnp.zeros((BLOCK, BLOCK), jnp.bfloat16)
    for b in range(col_blocks):
        tile[b, row_blocks] = zero
    for t in range(STEPS):
        near[t][CAP] = zero[:HALF]
        far[t][CAP] = zero[:HALF]
    for copy in tables:
        copy.wait()

    first = jnp.int32(4 * (row_blocks - 1))
    nxt[4 * row_blocks] = first
    for q in reversed(range(4 * row_blocks)):
        a, b = q // 4, q % 4
        if b < col_blocks:
            bit = mask[g * row_blocks + a, j * col_blocks + b]
            first = first + bit * (q - first)
        nxt[q] = first

    for load in loads:
        load.wait()

    q = nxt[0]
    for s in range(SPAN):
        packed[s] = tile[q & 3, q >> 2]
        q = nxt[q + 1]

    @pl.when(odd == 0)
    def _():
        pl.semaphore_signal(barrier, inc=1, device_id=at_grid_row(-2), device_id_type=MESH)

    pl.semaphore_wait(barrier, len(senders) + 1 - odd)

    def remote(src, dst, send, recv, device):
        return pltpu.make_async_remote_copy(
            src_ref=src, dst_ref=dst, send_sem=send, recv_sem=recv, device_id=device, device_id_type=MESH
        )

    def part(k):
        return pl.ds(k * SPAN, SPAN)

    def swap(n):
        blocks = pl.ds(0, SPAN) if n == 0 else pl.ds(SPAN, CAP - SPAN)
        return remote(packed.at[blocks, mate_rows], swapped.at[blocks], swap_s.at[n], swap_r.at[n], mate)

    def cross(k):
        return remote(chosen.at[part(k)], crossed.at[part(k)], cross_s.at[k], cross_r.at[k], across)

    def ring(t, k, by, sems):
        span = near[t].at[part(k)]
        return remote(span, span, sems.at[t, k], ring_r.at[t, k], at_plane(by))

    early = CHUNKS - 2

    def hand(t, late):
        blocks = pl.ds(early * SPAN, (CHUNKS - early) * SPAN) if late else pl.ds(0, early * SPAN)
        return remote(near[t].at[blocks], far[t].at[blocks], mate_s.at[t, late], mate_r.at[t, late], mate)

    slabs = [
        remote(r_send.at[t - 1], r_all.at[t], slab_s.at[t - 1], slab_r.at[t - 1], at_grid_row(-t))
        for t in range(1, STEPS)
    ]
    detours = lax.rem(g, 2) == 0
    detour = remote(r_send.at[STEPS - 2], passing.at[:], pass_s.at[0], pass_r, at_grid_row(2))
    onto = remote(passing.at[:], r_all.at[STEPS - 1], pass_s.at[1], slab_r.at[STEPS - 2], at_grid_row(STEPS - 1))

    @pl.when(is_source)
    def _():
        swap(0).start()

    for s in range(SPAN, CAP):
        packed[s] = tile[q & 3, q >> 2]
        q = nxt[q + 1]

    @pl.when(is_source)
    def _():
        swap(1).start()

    pick = owner[jnp.minimum(rel, STEPS - 1), g] & (sub - 1)

    for t in range(STEPS):
        slab = (owner[t, lax.rem(g - t + n_col, n_col)] & (sub - 1)) * col_blocks
        for a in range(col_blocks):
            for b in range(col_blocks):
                bit = mask[g * row_blocks + slab + a, j * col_blocks + b]
                block = tile[b, row_blocks + bit * (slab + a - row_blocks)]
                if t == 0:
                    r_all[0, a * BLOCK : (a + 1) * BLOCK, b * BLOCK : (b + 1) * BLOCK] = block
                else:
                    r_send[t - 1, a * BLOCK : (a + 1) * BLOCK, b * BLOCK : (b + 1) * BLOCK] = block

    mine = 1 - ((pick + core) & 1)

    def whole(flag):
        return jnp.full((SPAN, HALF, BLOCK), flag, jnp.int32).astype(jnp.float32).astype(jnp.bfloat16)

    @pl.when(is_source)
    def _():
        swap(0).wait_recv()
        own = whole(mine)

        @pl.loop(0, CHUNKS)
        def _(k):
            @pl.when(k == 1)
            def _():
                swap(1).wait_recv()

            chosen[part(k)] = packed[part(k), my_rows] * own + swapped[part(k)] * (1 - own)
            cross(k).start()

    slabs[1].start()
    slabs[0].start()

    @pl.when(detours)
    def _():
        detour.start()

    @pl.when(jnp.logical_not(detours))
    def _():
        slabs[2].start()


    for t in range(STEPS):
        at = owner[t, g] * col_blocks
        count = jnp.int32(0)
        for a in range(row_blocks):
            for b in range(col_blocks):
                bit = mask[g * row_blocks + a, at + b]
                slots[t, a * col_blocks + b] = CAP + bit * (count - CAP)
                count = count + bit
    out[...] = jnp.zeros_like(out)

    moved = whole(((pick >> 1) + place // 2) & 1)

    route = []
    for t in range(STEPS):
        above = lax.rem(rel - t + planes, planes)
        up = above <= UP[t]
        hops = jnp.where(up, above, planes - above)
        nearer = jnp.maximum(jnp.minimum(jnp.where(up, STEPS - 1 - t, t), hops - 1), 0)
        onward = (hops > 0) & (hops < jnp.where(up, UP[t], planes - 1 - UP[t]))
        route.append((up, onward, jnp.where(hops > 0, LAG * hops + SHIFT * nearer + AFTER, 0)))

    unit_rows = 2 * row_blocks // UNITS
    starts = [jnp.maximum(begin + CHUNKS, READY + t) for t, (_, _, begin) in enumerate(route)]
    ends = functools.reduce(jnp.maximum, [2 * STEPS * start + t for t, start in enumerate(starts)])

    def place_of(unit):
        half = lax.rem(core + unit // (UNITS // 2), 2)
        first_row = lax.rem(unit, UNITS // 2) * unit_rows
        return first_row, pl.ds(pl.multiple_of(half * HALF, HALF), HALF)

    def finished(unit):
        first_row, lines = place_of(unit)
        at = pl.ds(first_row, unit_rows)
        return pltpu.make_async_copy(out.at[at, lines], result.at[at, lines], out_sem.at[unit])


    @pl.loop(0, LAG * max(UP) + SHIFT * (STEPS - 1) + AFTER + CHUNKS + 1 + UNITS)
    def _(step):
        @pl.when(is_source & (step < CHUNKS))
        def _():
            cross(step).wait_recv()

        for t in range(STEPS):
            up, onward, begin = route[t]
            k = step - begin

            @pl.when((k >= 0) & (k < CHUNKS))
            def _():
                @pl.when(rel == t)
                def _():
                    near[t][part(k)] = chosen[part(k)] * (1 - moved) + crossed[part(k)] * moved
                    ring(t, k, 1, up_s).start()
                    ring(t, k, -1, down_s).start()

                @pl.when(rel != t)
                def _():
                    ring(t, k, 1, up_s).wait_recv()

                @pl.when(onward & up)
                def _():
                    ring(t, k, 1, up_s).start()

                @pl.when(onward & jnp.logical_not(up))
                def _():
                    ring(t, k, -1, down_s).start()

                @pl.when(k == early - 1)
                def _():
                    hand(t, 0).start()

                @pl.when(k == CHUNKS - 1)
                def _():
                    hand(t, 1).start()

        @pl.when(detours & (step == DETOUR))
        def _():
            detour.wait_recv()
            onto.start()

        for t in range(STEPS):
            unit = step - starts[t]

            @pl.when((unit >= 0) & (unit < UNITS))
            def _():
                @pl.when(unit == 0)
                def _():
                    if t > 0:
                        slabs[t - 1].wait_recv()

                @pl.when(unit == UNITS // 2)
                def _():
                    hand(t, 0).wait_recv()
                    hand(t, 1).wait_recv()

                first_row, lines = place_of(unit)
                for rows_of, chosen_half in ((near[t], unit < UNITS // 2), (far[t], unit >= UNITS // 2)):

                    @pl.when(chosen_half)
                    def _():
                        left = [
                            jnp.concatenate(
                                [rows_of[slots[t, (first_row + a) * col_blocks + b]] for b in range(col_blocks)],
                                axis=1,
                            )
                            for a in range(unit_rows)
                        ]
                        product = jnp.dot(
                            jnp.concatenate(left, axis=0), r_all[t], preferred_element_type=jnp.float32
                        )
                        out[pl.ds(first_row, unit_rows), lines] += product.reshape(unit_rows, HALF, width)

                @pl.when(ends == 2 * STEPS * starts[t] + t)
                def _():
                    finished(unit).start()

    @pl.when(is_source)
    def _():
        swap(0).wait_send()
        swap(1).wait_send()

        @pl.loop(0, CHUNKS)
        def _(k):
            cross(k).wait_send()

    for unit in range(UNITS):
        finished(unit).wait()

    slabs[0].wait_send()
    slabs[1].wait_send()

    @pl.when(detours)
    def _():
        detour.wait_send()
        onto.wait_send()

    @pl.when(jnp.logical_not(detours))
    def _():
        slabs[2].wait_send()

    for t in range(STEPS):
        up, onward, _ = route[t]
        hand(t, 0).wait_send()
        hand(t, 1).wait_send()

        @pl.when((rel == t) | (onward & up))
        def _():
            @pl.loop(0, CHUNKS)
            def _(k):
                ring(t, k, 1, up_s).wait_send()

        @pl.when((rel == t) | (onward & jnp.logical_not(up)))
        def _():
            @pl.loop(0, CHUNKS)
            def _(k):
                ring(t, k, -1, down_s).wait_send()


def shards(density, block_mask, owner):
    rows, width = density.shape
    row_blocks, col_blocks = rows // BLOCK, width // BLOCK
    n_row, n_col = lax.axis_size("row"), lax.axis_size("col")
    dma = pltpu.SemaphoreType.DMA
    bf16 = jnp.bfloat16
    piece = (CAP, HALF, BLOCK)
    operands = [
        pltpu.with_memory_space_constraint(operand, pltpu.HBM)
        for operand in (density.reshape(row_blocks, BLOCK, width), block_mask, owner)
    ]
    return pl.pallas_call(
        functools.partial(kernel, n_row, n_col),
        out_shape=jax.ShapeDtypeStruct((row_blocks, BLOCK, width), jnp.float32),
        in_specs=[pl.BlockSpec(memory_space=pltpu.HBM)] * 3,
        out_specs=pl.BlockSpec(memory_space=pl.ANY),
        scratch_shapes=[
            pltpu.SMEM(block_mask.shape, jnp.int32),
            pltpu.SMEM(owner.shape, jnp.int32),
            pltpu.VMEM((col_blocks, row_blocks + 1, BLOCK, BLOCK), bf16),
            pltpu.SMEM((4 * row_blocks + 1,), jnp.int32),
            pltpu.SMEM((STEPS, row_blocks * col_blocks), jnp.int32),
            pltpu.VMEM((CAP, BLOCK, BLOCK), bf16),
            pltpu.VMEM(piece, bf16),
            pltpu.VMEM(piece, bf16),
            pltpu.VMEM(piece, bf16),
            *[pltpu.VMEM((CAP + 1, HALF, BLOCK), bf16)] * (2 * STEPS),
            pltpu.VMEM((STEPS - 1, width, width), bf16),
            pltpu.VMEM((STEPS, width, width), bf16),
            pltpu.VMEM((width, width), bf16),
            pltpu.VMEM((row_blocks, BLOCK, width), jnp.float32),
            dma((col_blocks,)), dma((2,)), dma((2,)), dma((2,)), dma((CHUNKS,)), dma((CHUNKS,)),
            dma((STEPS, CHUNKS)), dma((STEPS, CHUNKS)), dma((STEPS, CHUNKS)),
            dma((STEPS, 2)), dma((STEPS, 2)),
            dma((STEPS - 1,)), dma((STEPS - 1,)), dma((2,)), dma, dma((UNITS,)),
        ],
        compiler_params=pltpu.CompilerParams(
            collective_id=0, has_side_effects=True, vmem_limit_bytes=48 * 1024 * 1024
        ),
        cost_estimate=pl.CostEstimate(
            flops=2 * rows * width * width * STEPS, bytes_accessed=rows * width * 6, transcendentals=0
        ),
        name="fox",
    )(*operands).reshape(rows, width)


def solution(mesh):
    placed = (P("col", "row"), P(), P())
    return jax.shard_map(
        shards, mesh=mesh, in_specs=placed, out_specs=P("col", "row"), check_vma=False
    )
```

```python
import functools

import jax
import jax.numpy as jnp
from jax import lax
from jax.experimental import pallas as pl
from jax.experimental.pallas import tpu as pltpu
from jax.sharding import PartitionSpec as P

BLOCK = 128
STEPS = 4
CAP = 21
HALF = BLOCK // 2
CHUNKS = 7
SPAN = CAP // CHUNKS
LAG = 4
SHIFT = 4
AFTER = 3
DETOUR = 12
READY = 18
UNITS = 4
UP = (3, 3, 4, 4)
MESH = pl.DeviceIdType.MESH


def kernel(
    n_row, n_col, density, mask_in, owner_in, result,
    mask, owner, tile, nxt, slots, packed, swapped, chosen, crossed, near_0, near_1, near_2, near_3, far_0, far_1, far_2, far_3, r_send, r_all, passing, out,
    load_sem, table_sem, swap_s, swap_r, cross_s, cross_r, up_s, down_s, ring_r, mate_s, mate_r, slab_s, slab_r, pass_s, pass_r, out_sem,
):
    near, far = (near_0, near_1, near_2, near_3), (far_0, far_1, far_2, far_3)
    g = lax.axis_index("col")
    j = lax.axis_index("row")
    sub = n_row // n_col
    planes = n_col
    plane = j // sub
    place = lax.rem(j, sub)
    core = lax.rem(place, 2)
    rel = lax.rem(plane - g + planes, planes)
    is_source = rel < STEPS
    row_blocks, _, width = density.shape
    col_blocks = width // BLOCK
    my_rows = pl.ds(pl.multiple_of(core * HALF, HALF), HALF)
    mate_rows = pl.ds(pl.multiple_of((1 - core) * HALF, HALF), HALF)

    def at_plane(by):
        return {"col": g, "row": lax.rem(plane + by + planes, planes) * sub + place}

    def at_grid_row(by):
        return {"col": lax.rem(g + by + n_col, n_col), "row": j}

    mate = {"col": g, "row": plane * sub + place + 1 - 2 * core}
    across = {"col": g, "row": plane * sub + lax.rem(place + 2, sub)}

    barrier = pltpu.get_barrier_semaphore()
    odd = lax.rem(g, 2)
    senders = [mate, across, at_plane(1), at_plane(-1), at_grid_row(1), at_grid_row(2)]
    senders += [at_grid_row(STEPS - 1 - 2 * (STEPS - 1) * odd)]
    for device in senders:
        pl.semaphore_signal(barrier, inc=1, device_id=device, device_id_type=MESH)

    tables = [
        pltpu.make_async_copy(mask_in, mask, table_sem.at[0]),
        pltpu.make_async_copy(owner_in, owner, table_sem.at[1]),
    ]
    loads = [
        pltpu.make_async_copy(
            density.at[:, :, pl.ds(b * BLOCK, BLOCK)], tile.at[b, pl.ds(0, row_blocks)], load_sem.at[b]
        )
        for b in range(col_blocks)
    ]
    for copy in tables + loads:
        copy.start()
    zero = jnp.zeros((BLOCK, BLOCK), jnp.bfloat16)
    for b in range(col_blocks):
        tile[b, row_blocks] = zero
    for t in range(STEPS):
        near[t][CAP] = zero[:HALF]
        far[t][CAP] = zero[:HALF]
    for copy in tables:
        copy.wait()

    first = jnp.int32(4 * (row_blocks - 1))
    nxt[4 * row_blocks] = first
    for q in reversed(range(4 * row_blocks)):
        a, b = q // 4, q % 4
        if b < col_blocks:
            bit = mask[g * row_blocks + a, j * col_blocks + b]
            first = first + bit * (q - first)
        nxt[q] = first

    for load in loads:
        load.wait()

    q = nxt[0]
    for s in range(SPAN):
        packed[s] = tile[q & 3, q >> 2]
        q = nxt[q + 1]

    @pl.when(odd == 0)
    def _():
        pl.semaphore_signal(barrier, inc=1, device_id=at_grid_row(-2), device_id_type=MESH)

    pl.semaphore_wait(barrier, len(senders) + 1 - odd)

    def remote(src, dst, send, recv, device):
        return pltpu.make_async_remote_copy(
            src_ref=src, dst_ref=dst, send_sem=send, recv_sem=recv, device_id=device, device_id_type=MESH
        )

    def part(k):
        return pl.ds(k * SPAN, SPAN)

    def swap(n):
        blocks = pl.ds(0, SPAN) if n == 0 else pl.ds(SPAN, CAP - SPAN)
        return remote(packed.at[blocks, mate_rows], swapped.at[blocks], swap_s.at[n], swap_r.at[n], mate)

    def cross(k):
        return remote(chosen.at[part(k)], crossed.at[part(k)], cross_s.at[k], cross_r.at[k], across)

    def ring(t, k, by, sems):
        span = near[t].at[part(k)]
        return remote(span, span, sems.at[t, k], ring_r.at[t, k], at_plane(by))

    early = CHUNKS - 2

    def hand(t, late):
        blocks = pl.ds(early * SPAN, (CHUNKS - early) * SPAN) if late else pl.ds(0, early * SPAN)
        return remote(near[t].at[blocks], far[t].at[blocks], mate_s.at[t, late], mate_r.at[t, late], mate)

    slabs = [
        remote(r_send.at[t - 1], r_all.at[t], slab_s.at[t - 1], slab_r.at[t - 1], at_grid_row(-t))
        for t in range(1, STEPS)
    ]
    detours = lax.rem(g, 2) == 0
    detour = remote(r_send.at[STEPS - 2], passing.at[:], pass_s.at[0], pass_r, at_grid_row(2))
    onto = remote(passing.at[:], r_all.at[STEPS - 1], pass_s.at[1], slab_r.at[STEPS - 2], at_grid_row(STEPS - 1))

    @pl.when(is_source)
    def _():
        swap(0).start()

    for s in range(SPAN, CAP):
        packed[s] = tile[q & 3, q >> 2]
        q = nxt[q + 1]

    @pl.when(is_source)
    def _():
        swap(1).start()

    pick = owner[jnp.minimum(rel, STEPS - 1), g] & (sub - 1)

    for t in range(STEPS):
        slab = (owner[t, lax.rem(g - t + n_col, n_col)] & (sub - 1)) * col_blocks
        for a in range(col_blocks):
            for b in range(col_blocks):
                bit = mask[g * row_blocks + slab + a, j * col_blocks + b]
                block = tile[b, row_blocks + bit * (slab + a - row_blocks)]
                if t == 0:
                    r_all[0, a * BLOCK : (a + 1) * BLOCK, b * BLOCK : (b + 1) * BLOCK] = block
                else:
                    r_send[t - 1, a * BLOCK : (a + 1) * BLOCK, b * BLOCK : (b + 1) * BLOCK] = block

    mine = 1 - ((pick + core) & 1)

    def whole(flag):
        return jnp.full((SPAN, HALF, BLOCK), flag, jnp.int32).astype(jnp.float32).astype(jnp.bfloat16)

    @pl.when(is_source)
    def _():
        swap(0).wait_recv()
        own = whole(mine)

        @pl.loop(0, CHUNKS)
        def _(k):
            @pl.when(k == 1)
            def _():
                swap(1).wait_recv()

            chosen[part(k)] = packed[part(k), my_rows] * own + swapped[part(k)] * (1 - own)
            cross(k).start()

    slabs[1].start()
    slabs[0].start()

    @pl.when(detours)
    def _():
        detour.start()

    @pl.when(jnp.logical_not(detours))
    def _():
        slabs[2].start()


    for t in range(STEPS):
        at = owner[t, g] * col_blocks
        count = jnp.int32(0)
        for a in range(row_blocks):
            for b in range(col_blocks):
                bit = mask[g * row_blocks + a, at + b]
                slots[t, a * col_blocks + b] = CAP + bit * (count - CAP)
                count = count + bit
    out[...] = jnp.zeros_like(out)

    moved = whole(((pick >> 1) + place // 2) & 1)

    route = []
    for t in range(STEPS):
        above = lax.rem(rel - t + planes, planes)
        up = above <= UP[t]
        hops = jnp.where(up, above, planes - above)
        nearer = jnp.maximum(jnp.minimum(jnp.where(up, STEPS - 1 - t, t), hops - 1), 0)
        onward = (hops > 0) & (hops < jnp.where(up, UP[t], planes - 1 - UP[t]))
        route.append((up, onward, jnp.where(hops > 0, LAG * hops + SHIFT * nearer + AFTER, 0)))

    unit_rows = 2 * row_blocks // UNITS
    starts = [jnp.maximum(begin + CHUNKS, READY + t) for t, (_, _, begin) in enumerate(route)]
    ends = functools.reduce(jnp.maximum, [2 * STEPS * start + t for t, start in enumerate(starts)])

    def place_of(unit):
        half = lax.rem(core + unit // (UNITS // 2), 2)
        first_row = lax.rem(unit, UNITS // 2) * unit_rows
        return first_row, pl.ds(pl.multiple_of(half * HALF, HALF), HALF)

    def finished(unit):
        first_row, lines = place_of(unit)
        at = pl.ds(first_row, unit_rows)
        return pltpu.make_async_copy(out.at[at, lines], result.at[at, lines], out_sem.at[unit])


    @pl.loop(0, LAG * max(UP) + SHIFT * (STEPS - 1) + AFTER + CHUNKS + 1 + UNITS)
    def _(step):
        @pl.when(is_source & (step < CHUNKS))
        def _():
            cross(step).wait_recv()

        for t in range(STEPS):
            up, onward, begin = route[t]
            k = step - begin

            @pl.when((k >= 0) & (k < CHUNKS))
            def _():
                @pl.when(rel == t)
                def _():
                    near[t][part(k)] = chosen[part(k)] * (1 - moved) + crossed[part(k)] * moved
                    ring(t, k, 1, up_s).start()
                    ring(t, k, -1, down_s).start()

                @pl.when(rel != t)
                def _():
                    ring(t, k, 1, up_s).wait_recv()

                @pl.when(onward & up)
                def _():
                    ring(t, k, 1, up_s).start()

                @pl.when(onward & jnp.logical_not(up))
                def _():
                    ring(t, k, -1, down_s).start()

                @pl.when(k == early - 1)
                def _():
                    hand(t, 0).start()

                @pl.when(k == CHUNKS - 1)
                def _():
                    hand(t, 1).start()

        @pl.when(detours & (step == DETOUR))
        def _():
            detour.wait_recv()
            onto.start()

        for t in range(STEPS):
            unit = step - starts[t]

            @pl.when((unit >= 0) & (unit < UNITS))
            def _():
                @pl.when(unit == 0)
                def _():
                    if t > 0:
                        slabs[t - 1].wait_recv()

                @pl.when(unit == UNITS // 2)
                def _():
                    hand(t, 0).wait_recv()
                    hand(t, 1).wait_recv()

                first_row, lines = place_of(unit)
                for rows_of, chosen_half in ((near[t], unit < UNITS // 2), (far[t], unit >= UNITS // 2)):

                    @pl.when(chosen_half)
                    def _():
                        left = [
                            jnp.concatenate(
                                [rows_of[slots[t, (first_row + a) * col_blocks + b]] for b in range(col_blocks)],
                                axis=1,
                            )
                            for a in range(unit_rows)
                        ]
                        product = jnp.dot(
                            jnp.concatenate(left, axis=0), r_all[t], preferred_element_type=jnp.float32
                        )
                        out[pl.ds(first_row, unit_rows), lines] += product.reshape(unit_rows, HALF, width)

                @pl.when(ends == 2 * STEPS * starts[t] + t)
                def _():
                    finished(unit).start()

    @pl.when(is_source)
    def _():
        swap(0).wait_send()
        swap(1).wait_send()

        @pl.loop(0, CHUNKS)
        def _(k):
            cross(k).wait_send()

    for unit in range(UNITS):
        finished(unit).wait()

    slabs[0].wait_send()
    slabs[1].wait_send()

    @pl.when(detours)
    def _():
        detour.wait_send()
        onto.wait_send()

    @pl.when(jnp.logical_not(detours))
    def _():
        slabs[2].wait_send()

    for t in range(STEPS):
        up, onward, _ = route[t]
        hand(t, 0).wait_send()
        hand(t, 1).wait_send()

        @pl.when((rel == t) | (onward & up))
        def _():
            @pl.loop(0, CHUNKS)
            def _(k):
                ring(t, k, 1, up_s).wait_send()

        @pl.when((rel == t) | (onward & jnp.logical_not(up)))
        def _():
            @pl.loop(0, CHUNKS)
            def _(k):
                ring(t, k, -1, down_s).wait_send()


def shards(density, block_mask, owner):
    rows, width = density.shape
    row_blocks, col_blocks = rows // BLOCK, width // BLOCK
    n_row, n_col = lax.axis_size("row"), lax.axis_size("col")
    dma = pltpu.SemaphoreType.DMA
    bf16 = jnp.bfloat16
    piece = (CAP, HALF, BLOCK)
    operands = [
        pltpu.with_memory_space_constraint(operand, pltpu.HBM)
        for operand in (density.reshape(row_blocks, BLOCK, width), block_mask, owner)
    ]
    return pl.pallas_call(
        functools.partial(kernel, n_row, n_col),
        out_shape=jax.ShapeDtypeStruct((row_blocks, BLOCK, width), jnp.float32),
        in_specs=[pl.BlockSpec(memory_space=pltpu.HBM)] * 3,
        out_specs=pl.BlockSpec(memory_space=pl.ANY),
        scratch_shapes=[
            pltpu.SMEM(block_mask.shape, jnp.int32),
            pltpu.SMEM(owner.shape, jnp.int32),
            pltpu.VMEM((col_blocks, row_blocks + 1, BLOCK, BLOCK), bf16),
            pltpu.SMEM((4 * row_blocks + 1,), jnp.int32),
            pltpu.SMEM((STEPS, row_blocks * col_blocks), jnp.int32),
            pltpu.VMEM((CAP, BLOCK, BLOCK), bf16),
            pltpu.VMEM(piece, bf16),
            pltpu.VMEM(piece, bf16),
            pltpu.VMEM(piece, bf16),
            *[pltpu.VMEM((CAP + 1, HALF, BLOCK), bf16)] * (2 * STEPS),
            pltpu.VMEM((STEPS - 1, width, width), bf16),
            pltpu.VMEM((STEPS, width, width), bf16),
            pltpu.VMEM((width, width), bf16),
            pltpu.VMEM((row_blocks, BLOCK, width), jnp.float32),
            dma((col_blocks,)), dma((2,)), dma((2,)), dma((2,)), dma((CHUNKS,)), dma((CHUNKS,)),
            dma((STEPS, CHUNKS)), dma((STEPS, CHUNKS)), dma((STEPS, CHUNKS)),
            dma((STEPS, 2)), dma((STEPS, 2)),
            dma((STEPS - 1,)), dma((STEPS - 1,)), dma((2,)), dma, dma((UNITS,)),
        ],
        compiler_params=pltpu.CompilerParams(
            collective_id=0, has_side_effects=True, vmem_limit_bytes=48 * 1024 * 1024
        ),
        cost_estimate=pl.CostEstimate(
            flops=2 * rows * width * width * STEPS, bytes_accessed=rows * width * 6, transcendentals=0
        ),
        name="fox",
    )(*operands).reshape(rows, width)


def solution(mesh):
    placed = (P("col", "row"), P(), P())
    return jax.shard_map(
        shards, mesh=mesh, in_specs=placed, out_specs=P("col", "row"), check_vma=False
    )
```
